512 devices in a mesh: rows: 16 (over y, z_hi), cols: 32 (over x, z_lo, core).
Axes of the slice: x: 4, y: 8, z: 8 (z_hi: 2, z_lo: 4; z = z_hi * 4 + z_lo), core: 2. Of those that a mesh axis runs over, the one named last changes fastest.
Arguments:
- pair: bfloat16 [1024, 1024, 128], P('rows', 'cols'), may hold values from -6 to 6
- length: int32 [1], replicated, may hold values from 256 to 1024
- ln_gain: float32 [128], replicated, may hold values from 0.25 to 1.75
- w_query: bfloat16 [128, 128], replicated, may hold values from -8 to 8
- w_key: bfloat16 [128, 128], replicated, may hold values from -8 to 8
- w_value: bfloat16 [128, 128], replicated, may hold values from -0.5 to 0.5
- w_gate: bfloat16 [128, 128], replicated, may hold values from -0.5 to 0.5
- w_bias: bfloat16 [128, 4], replicated, may hold values from -0.5 to 0.5
- w_out: bfloat16 [128, 128], replicated, may hold values from -0.5 to 0.5
- out_grad: bfloat16 [128, 1024, 128], P('rows', 'cols'), may hold values from -6 to 6
Outputs:
- update: bfloat16 [128, 1024, 128], P('rows', 'cols')
- pair_grad: float32 [1024, 1024, 128], P('rows', 'cols')
The draws below stay inside these ranges and needn't reach their ends.
Inputs may be any that keep to these rules, and one draw needn't show every extreme that they name: Keys at positions (length) and beyond are padding.
All inputs are finite; a program needn't handle non-finite values.
Results may differ from the reference program's by a relative error of at most 0.03.
The reference program's roundings to bfloat16 on the way count: a program that leaves them out, or rounds other values in their place, can miss the bound.
Values may be sent and summed in bfloat16 or wider, within the bound.
A program may use at most 64 MiB of HBM per device.

```python
import jax
import jax.numpy as jnp
from jax import lax

C = 128
H = 4
HD = 32
RI = 8
N = 1024
NI = 128
N_ROWS = 16


def shared_normal(key):
    return jax.random.normal(key, (C, C), jnp.float32)


def draw_w_query(key, part):
    shared = shared_normal(key)
    return (shared * C ** (-0.5)).astype(jnp.bfloat16)


def draw_w_key(key, part):
    key = jax.random.fold_in(key, 12)
    return (jax.random.normal(key, (C, C), jnp.float32) * C ** (-0.5)).astype(jnp.bfloat16)


def levels(rng, extent, pieces, smallest, high):
    level = 1.0
    for position, parts in pieces:
        heights = jax.random.uniform(jax.random.fold_in(jax.random.fold_in(rng, 6), position), (parts,), jnp.float32, smallest / len(pieces), high / len(pieces))
        level = level * jnp.repeat(jnp.exp(heights), extent[position] // parts).reshape((-1,) + (1,) * (len(extent) - 1 - position))
    return level


def normal_values(own_key, extent, deviation, limit, shards=(), kind=jnp.bfloat16):
    entries = deviation * jax.random.normal(own_key, extent, jnp.float32)
    if shards:
        entries = entries * levels(own_key, extent, shards, -0.22, 0.18)
    return jnp.clip(entries, -limit, limit).astype(kind)


def setup_inputs(seed: int = 0) -> dict:
    seeds = jax.random.split(jax.random.key(seed), 11)
    pair = normal_values(seeds[0], (N, N, C), 1.0, 6.0, ((0, 16), (1, 32)))
    length = jax.random.randint(seeds[1], (1,), N // 4, N + 1).astype(jnp.int32)
    ln_gain = jnp.clip(1.0 + 0.15 * jax.random.normal(seeds[2], (C,), jnp.float32), 0.25, 1.75)
    w_query = draw_w_query(jax.random.fold_in(seeds[10], 71), 0)
    w_key = draw_w_key(jax.random.fold_in(seeds[10], 71), 0)
    w_value = normal_values(seeds[5], (C, C), C ** -0.5, 0.5)
    w_gate = normal_values(seeds[6], (C, C), C ** -0.5, 0.5)
    w_bias = normal_values(seeds[7], (C, H), C ** -0.5, 0.5)
    w_out = normal_values(seeds[8], (C, C), C ** -0.5, 0.5)
    out_grad = normal_values(seeds[9], (NI, N, C), 1.0, 6.0, ((0, 16), (1, 32)))
    return dict(pair=pair, length=length, ln_gain=ln_gain, w_query=w_query, w_key=w_key, w_value=w_value, w_gate=w_gate, w_bias=w_bias, w_out=w_out, out_grad=out_grad)


EPS = 1e-05
NEG = -1000000000.0

def layer_norm(values, gain_vec):
    average = lax.optimization_barrier(jnp.mean(values, axis=-1, keepdims=True))
    centred = values - average
    variance = lax.optimization_barrier(jnp.mean(centred * centred, axis=-1, keepdims=True))
    return centred * lax.rsqrt(variance + EPS) * gain_vec

def project(inputs, weight):
    flat = inputs.reshape(-1, inputs.shape[-1])
    result = jnp.dot(flat, weight, preferred_element_type=jnp.float32)
    return result.reshape(inputs.shape[:-1] + (weight.shape[1],))

def round_trip(values):
    return lax.optimization_barrier(values.astype(jnp.bfloat16)).astype(jnp.float32)

def heads_of(values):
    return values.astype(jnp.float32).reshape(values.shape[:-1] + (H, HD))

def reference(pair, length, ln_gain, w_query, w_key, w_value, w_gate, w_bias, w_out, out_grad):
    score_scale = HD ** (-0.5)
    pair_f = pair.astype(jnp.float32)
    normed = layer_norm(pair_f, ln_gain).astype(jnp.bfloat16)
    bias = project(normed, w_bias).astype(jnp.bfloat16)
    bias_f = jnp.transpose(bias.astype(jnp.float32), (2, 0, 1))
    window = normed.reshape(N_ROWS, N // N_ROWS, N, C)[:, :RI].reshape(NI, N, C)
    query = (project(window, w_query) * score_scale).astype(jnp.bfloat16)
    keys = project(window, w_key).astype(jnp.bfloat16)
    value_proj = project(window, w_value).astype(jnp.bfloat16)
    gate = jax.nn.sigmoid(project(window, w_gate)).astype(jnp.bfloat16)
    keep = jnp.arange(N) < length[0]

    def logits_of(query_row, key_row):
        logits = jnp.einsum('jhd,khd->hjk', heads_of(query_row), heads_of(key_row)) + bias_f
        return jnp.where(keep[None, None, :], logits, NEG)

    def forward_row(row):
        query_row, key_row, value_row = row
        logits = logits_of(query_row, key_row)
        maxima = logits.max(-1)
        expo = jnp.exp(logits - maxima[..., None])
        totals = expo.sum(-1)
        attended = jnp.einsum('hjk,khd->jhd', round_trip(expo), heads_of(value_row))
        attended = attended / totals.T[..., None]
        return (attended.reshape(N, C), (maxima + jnp.log(totals)).T)
    attended, lse = lax.map(forward_row, (query, keys, value_proj))
    gate_f = gate.astype(jnp.float32)
    gated = (gate_f * attended).astype(jnp.bfloat16)
    update = project(gated, w_out).astype(jnp.bfloat16)
    grad_gated = project(out_grad, w_out.T)
    grad_attn = (grad_gated * gate_f).astype(jnp.bfloat16)
    grad_pre = grad_gated * attended * gate_f * (1.0 - gate_f)
    delta = lax.optimization_barrier(jnp.sum(heads_of(grad_attn) * heads_of(attended), -1))

    def backward_row(grad_bias, row):
        query_row, key_row, value_row, grad_row, lse_row, delta_row = row
        logits = logits_of(query_row, key_row)
        shares = jnp.exp(logits - lse_row.T[..., None])
        grad_shares = jnp.einsum('jhd,khd->hjk', heads_of(grad_row), heads_of(value_row))
        grad_logits = shares * (grad_shares - delta_row.T[..., None])
        rounded_grad = round_trip(grad_logits)
        grad_q = jnp.einsum('hjk,khd->jhd', rounded_grad, heads_of(key_row))
        grad_k = jnp.einsum('hjk,jhd->khd', rounded_grad, heads_of(query_row))
        grad_v = jnp.einsum('hjk,jhd->khd', round_trip(shares), heads_of(grad_row))
        outputs = (grad_q.reshape(N, C), grad_k.reshape(N, C), grad_v.reshape(N, C))
        return (grad_bias + grad_logits, outputs)
    grad_bias, (grad_q, grad_k, grad_v) = lax.scan(backward_row, jnp.zeros((H, N, N), jnp.float32), (query, keys, value_proj, grad_attn, lse, delta))
    combined = jnp.concatenate([(grad_q * score_scale).astype(jnp.bfloat16), grad_k.astype(jnp.bfloat16), grad_v.astype(jnp.bfloat16), grad_pre.astype(jnp.bfloat16)], axis=-1)
    stacked = jnp.concatenate([w_query, w_key, w_value, w_gate], axis=1)
    grad_window = project(combined, stacked.T)
    grad_normed = jnp.einsum('hij,ch->ijc', grad_bias, w_bias.astype(jnp.float32), precision=lax.Precision.HIGHEST)
    grad_normed = grad_normed.reshape(N_ROWS, N // N_ROWS, N, C)
    grad_normed = grad_normed.at[:, :RI].add(grad_window.reshape(N_ROWS, RI, N, C)).reshape(N, N, C)
    unused, pullback = jax.vjp(lambda inputs: layer_norm(inputs, ln_gain), pair_f)
    pair_grad = pullback(grad_normed)[0]
    return (update, pair_grad)
```

```python
import jax
import jax.numpy as jnp
from jax import lax
from jax.experimental import pallas as pl
from jax.experimental.pallas import tpu as pltpu
from jax.sharding import PartitionSpec as P

EPS = 1e-05
NEG = -1000000000.0
MESH = pl.DeviceIdType.MESH
f32 = jnp.float32
bf16 = jnp.bfloat16


def nn(left, right):
    return lax.dot_general(left, right, (((1,), (0,)), ((), ())), preferred_element_type=f32)


def nt(left, right):
    return lax.dot_general(left, right, (((1,), (1,)), ((), ())), preferred_element_type=f32)


def lane_block(shape):
    return lax.shift_right_logical(lax.broadcasted_iota(jnp.int32, shape, len(shape) - 1), 5)


def lane_swap(tiles):
    block = lane_block(tiles[0].shape)
    outs = []
    for i in range(4):
        acc = None
        for b in range(4):
            shift = (32 * (b - i)) % 128
            moved = tiles[b] if shift == 0 else pltpu.roll(tiles[b], shift, 1)
            acc = moved if acc is None else jnp.where(block == b, moved, acc)
        outs.append(acc)
    return outs


def remote(src, dst, send_sem, recv_sem, device):
    return pltpu.make_async_remote_copy(
        src_ref=src, dst_ref=dst, send_sem=send_sem, recv_sem=recv_sem,
        device_id=device, device_id_type=MESH,
    )


def kernel(
    pair, length, gain, w_query, w_key, w_value, w_gate, w_bias, w_out, out_grad,
    update, pair_grad,
    xhat, rstd_all, w_rows, gate_s, gg_s, zsend, kv, qd, qdt, bsend, brecv, grid, bias, bias_f,
    dbias, att, dqkv, db_send, db_x, db_y, db_t, db_h, db_out, db_in, dkv_send, dkv_in,
    e_in, o_in, gw,
    kvz_s, kvz_r, qdz_s, qdz_r, bz_s, bz_r, kvx_s, kvx_r, kvc_s, kvc_r, bh_s, bh_r,
    by_s, by_r, by2_s, by2_r, bx_s, bx_r, dbx_s, dbx_r, dby_s, dby_r, dbh_s, dbh_r,
    dbz_s, dbz_r, dkvx_s, dkvx_r, oz_s, oz_r, dqz_s, dqz_r, dkvz_s, dkvz_r,
):
    row = lax.axis_index("rows")
    col = lax.axis_index("cols")
    y, zhi = lax.div(row, 2), lax.rem(row, 2)
    x, z, core = lax.div(col, 8), lax.rem(lax.div(col, 2), 4), lax.rem(col, 2)
    blk = x * 2 + core
    other = 1 - core

    def device(row_, x_, z_, core_):
        return {"rows": row_, "cols": x_ * 8 + z_ * 2 + core_}

    def z_at(d):
        return lax.rem(z + d, 4)

    def z_dev(d):
        return device(row, x, z_at(d), core)

    def x_at(d):
        return lax.rem(x + d, 4)

    def x_dev(d):
        return device(row, x_at(d), z, core)

    def blk_at(d):
        return lax.rem(blk + d, 8)

    def blk_dev(d):
        return device(row, lax.div(blk_at(d), 2), z, lax.rem(blk_at(d), 2))

    def y_at(d):
        return lax.rem(y + d, 8)

    def y_dev(d):
        return device(y_at(d) * 2 + zhi, x, z, core)

    core_dev = device(row, x, z, other)
    h_dev = device(y * 2 + 1 - zhi, x, z, core)
    me_dev = core_dev

    sent = []

    def send(src, dst, send_sem, recv_sem, dev):
        copy = remote(src, dst, send_sem, recv_sem, dev)
        copy.start()
        sent.append(copy)

    def arrived(slot, send_sem, recv_sem):
        remote(slot, slot, send_sem, recv_sem, me_dev).wait_recv()

    barrier = pltpu.get_barrier_semaphore()
    partners = (
        [z_dev(d) for d in (1, 2, 3)] + [blk_dev(d) for d in range(1, 8)]
        + [y_dev(d) for d in range(1, 8)] + [h_dev]
    )
    for dev in partners:
        pl.semaphore_signal(barrier, inc=1, device_id=dev, device_id_type=MESH)

    gain_v = gain[...]

    def norm(values):
        average = jnp.mean(values, axis=-1, keepdims=True)
        centred = values - average
        variance = jnp.mean(centred * centred, axis=-1, keepdims=True)
        rstd = lax.rsqrt(variance + EPS)
        return centred * rstd, rstd, centred

    win = pair[0:8].reshape(256, 128).astype(f32)
    hat, _, _ = norm(win)
    window = (hat * gain_v).astype(bf16)
    query = (nn(window, w_query[...]) * (32 ** (-0.5))).astype(bf16).astype(f32)
    keys = nn(window, w_key[...]).astype(bf16).astype(f32)
    vals = nn(window, w_value[...]).astype(bf16).astype(f32)
    gate = jax.nn.sigmoid(nn(window, w_gate[...])).astype(bf16).astype(f32)
    gg = nt(out_grad[...].reshape(256, 128), w_out[...])
    ga = (gg * gate).astype(bf16).astype(f32)
    gate_s[...] = gate
    gg_s[...] = gg
    for n, array in enumerate((keys, vals, query, ga)):
        for g in range(2):
            outs = lane_swap([array[(g * 4 + b) * 32:(g * 4 + b + 1) * 32] for b in range(4)])
            for h in range(4):
                zsend[h, n, g] = outs[h].astype(bf16)

    pl.semaphore_wait(barrier, len(partners))

    z_rows = pl.ds(pl.multiple_of(z * 32, 32), 32)
    for d in (1, 3, 2):
        send(zsend.at[z_at(d), 0:2], kv.at[blk, :, :, z_rows, :], kvz_s.at[d], kvz_r.at[d], z_dev(d))
    for d in (1, 3, 2):
        send(zsend.at[z_at(d), 2:4], qd.at[:, :, z_rows, :], qdz_s.at[d], qdz_r.at[d], z_dev(d))
    kv[blk, :, :, z_rows, :] = zsend[z, 0:2]
    qd[:, :, z_rows, :] = zsend[z, 2:4]

    pick = lax.broadcasted_iota(jnp.int32, (64, 4), 0) // 16 == lax.broadcasted_iota(
        jnp.int32, (64, 4), 1)
    w_rows[...] = nt(pick.astype(bf16), w_bias[...]).astype(bf16)
    row_in = lax.rem(lax.broadcasted_iota(jnp.int32, (64, 128), 0), 16)

    def tile_step(i, acc):
        for u in range(4):
            jj = i * 4 + u
            tokens = jnp.concatenate([pair[q * 16 + jj] for q in range(4)], axis=0).astype(f32)
            hat, rstd, _ = norm(tokens)
            xhat[jj] = hat
            rstd_all[jj] = jnp.broadcast_to(rstd, (128, 128))
            normed = (hat * gain_v).astype(bf16)
            chosen = jnp.where(row_in == jj, w_rows[...].astype(f32), 0.0).astype(bf16)
            acc = acc + nt(chosen, normed)
        return acc

    tile_bias = lax.fori_loop(0, 4, tile_step, jnp.zeros((64, 128), f32))
    bsend[...] = tile_bias.astype(bf16).reshape(4, 16, 128)
    for d in (1, 3, 2):
        send(bsend.at[z_at(d)], brecv.at[z], bz_s.at[d], bz_r.at[d], z_dev(d))
    brecv[z] = bsend[z]

    for d in (1, 2, 3):
        rows_d = pl.ds(pl.multiple_of(z_at(4 - d) * 32, 32), 32)
        arrived(kv.at[blk, :, :, rows_d, :], kvz_s.at[d], kvz_r.at[d])
    for d in (1, 3, 2):
        send(kv.at[blk], kv.at[blk], kvx_s.at[d], kvx_r.at[d], x_dev(d))
    send(kv.at[blk], kv.at[blk], kvc_s.at[0], kvc_r.at[0], core_dev)

    for d in (1, 2, 3):
        arrived(brecv.at[z_at(4 - d)], bz_s.at[d], bz_r.at[d])
    outs = lane_swap([brecv[b].astype(f32) for b in range(4)])
    for q in range(4):
        grid[row, q * 16:(q + 1) * 16] = outs[q].astype(bf16)
    send(grid.at[row], grid.at[row], bh_s.at[0], bh_r.at[0], h_dev)
    for d in (1, 7, 2, 6, 3, 5, 4):
        send(grid.at[row], grid.at[row], by_s.at[d], by_r.at[d], y_dev(d))
    row_h = y * 2 + 1 - zhi
    arrived(grid.at[row_h], bh_s.at[0], bh_r.at[0])
    for d in (1, 7, 2, 6, 3, 5, 4):
        send(grid.at[row_h], grid.at[row_h], by2_s.at[d], by2_r.at[d], y_dev(d))

    for d in (1, 2, 3):
        rows_d = pl.ds(pl.multiple_of(z_at(4 - d) * 32, 32), 32)
        arrived(qd.at[:, :, rows_d, :], qdz_s.at[d], qdz_r.at[d])
    for n in range(2):
        for g in range(2):
            qdt[n, g] = qd[n, g].astype(f32).T.astype(bf16)

    for d in range(1, 8):
        arrived(grid.at[y_at(8 - d) * 2 + zhi], by_s.at[d], by_r.at[d])
        arrived(grid.at[y_at(8 - d) * 2 + 1 - zhi], by2_s.at[d], by2_r.at[d])
    for d in (1, 7, 2, 6, 3, 5, 4):
        to = blk_at(d)
        part = grid.at[
            pl.ds(pl.multiple_of(lax.div(to, 2) * 4, 4), 4),
            pl.ds(pl.multiple_of(lax.rem(to, 2) * 32, 32), 32), :]
        send(part, bias.at[blk], bx_s.at[d], bx_r.at[d], blk_dev(d))
    bias[blk] = grid[pl.ds(pl.multiple_of(x * 4, 4), 4), pl.ds(pl.multiple_of(core * 32, 32), 32), :]

    for d in (1, 3, 2):
        blk_d = x_at(4 - d) * 2 + core
        arrived(kv.at[blk_d], kvx_s.at[d], kvx_r.at[d])
        send(kv.at[blk_d], kv.at[blk_d], kvc_s.at[d], kvc_r.at[d], core_dev)
    for d in (0, 1, 3, 2):
        arrived(kv.at[x_at(4 - d) * 2 + other], kvc_s.at[d], kvc_r.at[d])
    for d in range(1, 8):
        arrived(bias.at[blk_at(8 - d)], bx_s.at[d], bx_r.at[d])

    spot = lax.broadcasted_iota(jnp.int32, (1, 1024), 1)
    spot_c = (lax.div(spot, 256) * 8 + lax.rem(lax.div(spot, 32), 4) * 2
              + lax.rem(lax.div(spot, 128), 2))
    keep = spot_c * 32 + lax.rem(spot, 32) < length[0]
    for b in range(8):
        bias_f[:, b * 128:(b + 1) * 128] = bias[b].reshape(128, 128).astype(f32)
    dbias[...] = jnp.zeros_like(dbias)
    att[...] = jnp.zeros_like(att)
    dqkv[0] = jnp.zeros_like(dqkv[0])
    lanes = lane_block((128, 128))

    for g in range(2):
        def attend(a, carry):
            own = lanes == a
            key = kv[:, 0, g].reshape(1024, 128)
            value = kv[:, 1, g].reshape(1024, 128)
            q_a = jnp.where(own, qd[0, g].astype(f32), 0.0).astype(bf16)
            do_f = jnp.where(own, qd[1, g].astype(f32), 0.0)
            do_a = do_f.astype(bf16)
            logits = jnp.where(keep, nt(q_a, key) + bias_f[...], NEG)
            top = jnp.max(logits, axis=-1, keepdims=True)
            expo = jnp.exp(logits - top)
            inv = 1.0 / jnp.sum(expo, axis=-1, keepdims=True)
            out = nn(expo.astype(bf16), value) * inv
            out = jnp.where(own, out, 0.0)
            att[g] = att[g] + out
            delta = jnp.sum(do_f * out, axis=-1, keepdims=True)
            shares = expo * inv
            grads = shares * (nt(do_a, value) - delta)
            dbias[...] = dbias[...] + grads
            grads_b = grads.astype(bf16)
            dq = nn(grads_b, key) * (32 ** (-0.5))
            dqkv[0, g] = jnp.where(own, dq, dqkv[0, g].astype(f32)).astype(bf16)
            part = pl.ds(pl.multiple_of(a * 32, 32), 32)
            dk = nn(qdt[0, g, part, :], grads_b).astype(bf16)
            dv = nn(qdt[1, g, part, :], shares.astype(bf16)).astype(bf16)
            for b in range(8):
                dkv_send[b, 0, g, part, :] = dk[:, b * 128:(b + 1) * 128]
                dkv_send[b, 1, g, part, :] = dv[:, b * 128:(b + 1) * 128]
            return carry

        lax.fori_loop(0, 4, attend, 0)

    for b in range(8):
        db_send[b] = dbias[:, b * 128:(b + 1) * 128].astype(bf16)
    for d in (1, 7, 2, 6, 3, 5, 4):
        send(db_send.at[blk_at(d)], db_x.at[blk], dbx_s.at[d], dbx_r.at[d], blk_dev(d))
    for d in (1, 7, 2, 6, 3, 5, 4):
        send(dkv_send.at[blk_at(d)], dkv_in.at[blk], dkvx_s.at[d], dkvx_r.at[d], blk_dev(d))
    for d in (1, 3, 2):
        rows_d = pl.ds(pl.multiple_of(z_at(d) * 32, 32), 32)
        send(att.at[:, rows_d, :], o_in.at[z], oz_s.at[d], oz_r.at[d], z_dev(d))
        send(dqkv.at[0, :, rows_d, :], e_in.at[z, 0], dqz_s.at[d], dqz_r.at[d], z_dev(d))
    db_x[blk] = db_send[blk]
    dkv_in[blk] = dkv_send[blk]
    o_in[z] = att[:, z_rows, :]
    e_in[z, 0] = dqkv[0, :, z_rows, :]

    for d in range(1, 8):
        arrived(db_x.at[blk_at(8 - d)], dbx_s.at[d], dbx_r.at[d])

    def y_part(to):
        return (pl.ds(pl.multiple_of(lax.div(to, 2) * 2, 2), 2),
                pl.ds(pl.multiple_of(lax.rem(to, 2) * 64, 64), 64))

    for d in (1, 7, 2, 6, 3, 5, 4):
        blks, js = y_part(y_at(d))
        send(db_x.at[blks, js, :], db_y.at[y], dby_s.at[d], dby_r.at[d], y_dev(d))
    blks, js = y_part(y)
    db_y[y] = db_x[blks, js, :]

    for d in range(1, 8):
        arrived(db_y.at[y_at(8 - d)], dby_s.at[d], dby_r.at[d])
    total = db_y[0].astype(f32)
    for b in range(1, 8):
        total = total + db_y[b].astype(f32)
    db_t[...] = total
    theirs = pl.ds(pl.multiple_of((1 - zhi) * 32, 32), 32)
    mine = pl.ds(pl.multiple_of(zhi * 32, 32), 32)
    send(db_t.at[:, theirs, :], db_h, dbh_s.at[0], dbh_r.at[0], h_dev)

    for d in range(1, 8):
        arrived(dkv_in.at[blk_at(8 - d)], dkvx_s.at[d], dkvx_r.at[d])
    for n in range(2):
        for g in range(2):
            total = dkv_in[0, n, g].astype(f32)
            for b in range(1, 8):
                total = total + dkv_in[b, n, g].astype(f32)
            dqkv[1 + n, g] = total.T.astype(bf16)
    for d in (1, 3, 2):
        rows_d = pl.ds(pl.multiple_of(z_at(d) * 32, 32), 32)
        send(dqkv.at[1:3, :, rows_d, :], e_in.at[z, 1:3], dkvz_s.at[d], dkvz_r.at[d], z_dev(d))
    e_in[z, 1:3] = dqkv[1:3, :, z_rows, :]

    arrived(db_h, dbh_s.at[0], dbh_r.at[0])
    final = (db_t[:, mine, :] + db_h[...]).reshape(64, 128)
    outs = lane_swap([final[q * 16:(q + 1) * 16] for q in range(4)])
    for b in range(4):
        db_out[b] = outs[b]
    for d in (1, 3, 2):
        send(db_out.at[z_at(d)], db_in.at[z], dbz_s.at[d], dbz_r.at[d], z_dev(d))
    db_in[z] = db_out[z]

    for d in (1, 2, 3):
        h_d = z_at(4 - d)
        arrived(o_in.at[h_d], oz_s.at[d], oz_r.at[d])
        arrived(e_in.at[h_d, 0], dqz_s.at[d], dqz_r.at[d])
    gated = []
    pres = []
    for g in range(2):
        outs = lane_swap([o_in[h, g] for h in range(4)])
        for i in range(4):
            at = slice((g * 4 + i) * 32, (g * 4 + i + 1) * 32)
            gate_t, gg_t = gate_s[at], gg_s[at]
            gated.append((gate_t * outs[i]).astype(bf16))
            pres.append((gg_t * outs[i] * gate_t * (1.0 - gate_t)).astype(bf16))
    update[...] = nn(jnp.concatenate(gated, axis=0), w_out[...]).astype(bf16).reshape(8, 32, 128)
    for d in (1, 2, 3):
        arrived(e_in.at[z_at(4 - d), 1:3], dkvz_s.at[d], dkvz_r.at[d])
    sides = [jnp.concatenate(pres, axis=0)]
    for n in range(3):
        tiles = []
        for g in range(2):
            tiles += lane_swap([e_in[h, n, g].astype(f32) for h in range(4)])
        sides.append(jnp.concatenate(tiles, axis=0).astype(bf16))
    grad_window = (nt(sides[1], w_query[...]) + nt(sides[2], w_key[...])
                   + nt(sides[3], w_value[...]) + nt(sides[0], w_gate[...]))
    gw[0:8] = grad_window.reshape(8, 32, 128)
    gw[8:16] = jnp.zeros((8, 32, 128), f32)

    for d in (1, 2, 3):
        arrived(db_in.at[z_at(4 - d)], dbz_s.at[d], dbz_r.at[d])
    flat = db_in[...].reshape(64, 128).T
    high = flat.astype(bf16)
    rest = flat - high.astype(f32)
    mid = rest.astype(bf16)
    low = (rest - mid.astype(f32)).astype(bf16)

    def final_step(i, carry):
        for u in range(2):
            jj = i * 2 + u
            chosen = jnp.where(row_in == jj, w_rows[...].astype(f32), 0.0).astype(bf16)
            grad = nn(high, chosen) + (nn(mid, chosen) + nn(low, chosen))
            grad = jnp.concatenate([grad[0:32] + gw[jj], grad[32:]], axis=0) * gain_v
            hat = xhat[jj]
            first = jnp.mean(grad, axis=-1, keepdims=True)
            second = jnp.mean(grad * hat, axis=-1, keepdims=True)
            result = rstd_all[jj] * (grad - first - hat * second)
            for q in range(4):
                pair_grad[q * 16 + jj] = result[q * 32:(q + 1) * 32]
        return carry

    lax.fori_loop(0, 8, final_step, 0)

    for copy in sent:
        copy.wait_send()


def body(pair, length, ln_gain, w_query, w_key, w_value, w_gate, w_bias, w_out, out_grad):
    vmem = pl.BlockSpec(memory_space=pltpu.VMEM)
    smem = pl.BlockSpec(memory_space=pltpu.SMEM)

    def dma(n):
        return [pltpu.SemaphoreType.DMA((n,)), pltpu.SemaphoreType.DMA((n,))]

    scratch = [
        pltpu.VMEM((16, 128, 128), f32),
        pltpu.VMEM((16, 128, 128), f32),
        pltpu.VMEM((64, 128), bf16),
        pltpu.VMEM((256, 128), f32),
        pltpu.VMEM((256, 128), f32),
        pltpu.VMEM((4, 4, 2, 32, 128), bf16),
        pltpu.VMEM((8, 2, 2, 128, 128), bf16),
        pltpu.VMEM((2, 2, 128, 128), bf16),
        pltpu.VMEM((2, 2, 128, 128), bf16),
        pltpu.VMEM((4, 16, 128), bf16),
        pltpu.VMEM((4, 16, 128), bf16),
        pltpu.VMEM((16, 64, 128), bf16),
        pltpu.VMEM((8, 4, 32, 128), bf16),
        pltpu.VMEM((128, 1024), f32),
        pltpu.VMEM((128, 1024), f32),
        pltpu.VMEM((2, 128, 128), f32),
        pltpu.VMEM((3, 2, 128, 128), bf16),
        pltpu.VMEM((8, 128, 128), bf16),
        pltpu.VMEM((8, 128, 128), bf16),
        pltpu.VMEM((8, 2, 64, 128), bf16),
        pltpu.VMEM((2, 64, 128), f32),
        pltpu.VMEM((2, 32, 128), f32),
        pltpu.VMEM((4, 16, 128), f32),
        pltpu.VMEM((4, 16, 128), f32),
        pltpu.VMEM((8, 2, 2, 128, 128), bf16),
        pltpu.VMEM((8, 2, 2, 128, 128), bf16),
        pltpu.VMEM((4, 3, 2, 32, 128), bf16),
        pltpu.VMEM((4, 2, 32, 128), f32),
        pltpu.VMEM((16, 32, 128), f32),
    ]
    for n in (4, 4, 4, 4, 4, 1, 8, 8, 8, 8, 8, 1, 4, 8, 4, 4, 4):
        scratch += dma(n)
    call = pl.pallas_call(
        kernel,
        out_shape=(
            jax.ShapeDtypeStruct(out_grad.shape, bf16),
            jax.ShapeDtypeStruct(pair.shape, f32),
        ),
        in_specs=[vmem, smem] + [vmem] * 8,
        out_specs=(vmem, vmem),
        scratch_shapes=scratch,
        compiler_params=pltpu.CompilerParams(
            collective_id=0, has_side_effects=True, vmem_limit_bytes=48 * 1024 * 1024
        ),
    )
    return call(
        pair, length, ln_gain.reshape(1, 128), w_query, w_key, w_value, w_gate, w_bias, w_out,
        out_grad,
    )


def solution(mesh):
    tiled = P("rows", "cols", None)
    placed = (tiled, P(), P(), P(), P(), P(), P(), P(), P(), tiled)
    return jax.shard_map(
        body, mesh=mesh, in_specs=placed, out_specs=(tiled, tiled), check_vma=False
    )
```

```python
import jax
import jax.numpy as jnp
from jax import lax
from jax.experimental import pallas as pl
from jax.experimental.pallas import tpu as pltpu
from jax.sharding import PartitionSpec as P

EPS = 1e-05
NEG = -1000000000.0
MESH = pl.DeviceIdType.MESH
f32 = jnp.float32
bf16 = jnp.bfloat16
COPIES = (
    ("kvz", 4), ("qdz", 4), ("bz", 8), ("kva", 4), ("kvb", 2), ("kvc", 4), ("bt", 2), ("ya", 8),
    ("yb", 2), ("dkvc", 2), ("dr", 4), ("df", 8), ("yr", 4), ("yd", 4), ("dt", 2), ("dbz", 8),
    ("oz", 4), ("dqz", 4), ("dkvz", 4),
)


def nn(left, right):
    return lax.dot_general(left, right, (((1,), (0,)), ((), ())), preferred_element_type=f32)


def nt(left, right):
    return lax.dot_general(left, right, (((1,), (1,)), ((), ())), preferred_element_type=f32)


def lane_block(shape):
    return lax.shift_right_logical(lax.broadcasted_iota(jnp.int32, shape, len(shape) - 1), 5)


def lane_swap(tiles):
    block = lane_block(tiles[0].shape)
    outs = []
    for i in range(4):
        acc = None
        for b in range(4):
            shift = (32 * (b - i)) % 128
            moved = tiles[b] if shift == 0 else pltpu.roll(tiles[b], shift, 1)
            acc = moved if acc is None else jnp.where(block == b, moved, acc)
        outs.append(acc)
    return outs


def remote(src, dst, send_sem, recv_sem, device):
    return pltpu.make_async_remote_copy(
        src_ref=src, dst_ref=dst, send_sem=send_sem, recv_sem=recv_sem,
        device_id=device, device_id_type=MESH,
    )


def kernel(
    pair_h, length, gain, w_query_h, w_key_h, w_value_h, w_gate_h, w_bias, w_out_h, out_grad_h,
    update, pair_grad,
    pair, w_query, w_key, w_value, w_gate, w_out, out_grad, load_sem, xhat, rstd_all, w_rows, gate_s, gg_s, zsend, kv, qd, qdt, bsend, brecv, grid, bias, bias_f,
    dbias, att, dqkv, db_send, db_r, db_rh, db_2, db_y, db_s, db_t, db_out, db_in,
    dkv_send, dkv_c, dkv_m, dkv_r, dkv_2, dkv_in,
    e_in, o_in, gw,
    *sems,
):
    sem = {name: sems[2 * n:2 * n + 2] for n, (name, _) in enumerate(COPIES)}
    row = lax.axis_index("rows")
    col = lax.axis_index("cols")
    y, zhi = lax.div(row, 2), lax.rem(row, 2)
    x, z, core = lax.div(col, 8), lax.rem(lax.div(col, 2), 4), lax.rem(col, 2)
    blk = x * 2 + core
    other = 1 - core

    def device(row_, x_, z_, core_):
        return {"rows": row_, "cols": x_ * 8 + z_ * 2 + core_}

    def z_at(d):
        return lax.rem(z + d, 4)

    def z_dev(d):
        return device(row, x, z_at(d), core)

    def zz_dev(e, d):
        return device(y * 2 + lax.rem(zhi + e, 2), x, z_at(d), core)

    def x_at(d):
        return lax.rem(x + d, 4)

    def x_dev(d):
        return device(row, x_at(d), z, core)

    def y_at(d):
        return lax.rem(y + d, 8)

    def y_dev(d):
        return device(y_at(d) * 2 + zhi, x, z, core)

    def by_column(c):
        return device(blk * 2 + zhi, lax.div(y, 2), z, c)

    def by_row(s):
        return device((x * 2 + s) * 2 + zhi, lax.div(y, 2), z, lax.rem(y, 2))

    core_dev = device(row, x, z, other)
    stays = blk == y

    sent = []
    turned = []

    def send(src, dst, name, n, dev, at=None):
        copy = remote(src, dst, sem[name][0].at[n], sem[name][1].at[n if at is None else at], dev)
        copy.start()
        sent.append(copy)

    def turn(src, dst, name, at, dev):
        away = remote(src, dst, sem[name][0].at[0], sem[name][1].at[at], dev)
        here = pltpu.make_async_copy(src, dst, sem[name][1].at[at])

        @pl.when(stays)
        def _():
            here.start()

        @pl.when(jnp.logical_not(stays))
        def _():
            away.start()

        turned.append(away)

    def arrived(slot, name, n):
        remote(slot, slot, sem[name][0].at[n], sem[name][1].at[n], core_dev).wait_recv()

    loads = [
        pltpu.make_async_copy(src, dst, load_sem.at[n])
        for n, (src, dst) in enumerate((
            (pair_h, pair), (w_query_h, w_query), (w_key_h, w_key), (w_value_h, w_value),
            (w_gate_h, w_gate), (w_out_h, w_out), (out_grad_h, out_grad)))
    ]
    for copy in loads:
        copy.start()

    barrier = pltpu.get_barrier_semaphore()
    partners = (
        [zz_dev(e, d) for e in range(2) for d in range(4) if (e, d) != (0, 0)]
        + [core_dev, x_dev(1), x_dev(3)] + [y_dev(d) for d in (1, 7, 2, 6)]
        + [by_column(other), by_row(other)]
    )

    def greet(dev):
        pl.semaphore_signal(barrier, inc=1, device_id=dev, device_id_type=MESH)

    for dev in partners:
        greet(dev)

    @pl.when(jnp.logical_not(stays))
    def _():
        greet(by_column(core))
        greet(by_row(core))

    gain_v = gain[...]
    for copy in loads:
        copy.wait()

    def norm(values):
        average = jnp.mean(values, axis=-1, keepdims=True)
        centred = values - average
        variance = jnp.mean(centred * centred, axis=-1, keepdims=True)
        rstd = lax.rsqrt(variance + EPS)
        return centred * rstd, rstd, centred

    win = pair[0:8].reshape(256, 128).astype(f32)
    hat, _, _ = norm(win)
    window = (hat * gain_v).astype(bf16)
    query = (nn(window, w_query[...]) * (32 ** (-0.5))).astype(bf16).astype(f32)
    keys = nn(window, w_key[...]).astype(bf16).astype(f32)
    vals = nn(window, w_value[...]).astype(bf16).astype(f32)
    gate = jax.nn.sigmoid(nn(window, w_gate[...])).astype(bf16).astype(f32)
    gg = nt(out_grad[...].reshape(256, 128), w_out[...])
    ga = (gg * gate).astype(bf16).astype(f32)
    gate_s[...] = gate
    gg_s[...] = gg
    for n, array in enumerate((keys, vals, query, ga)):
        for g in range(2):
            outs = lane_swap([array[(g * 4 + b) * 32:(g * 4 + b + 1) * 32] for b in range(4)])
            for h in range(4):
                zsend[h, n, g] = outs[h].astype(bf16)

    pl.semaphore_wait(barrier, len(partners) + jnp.where(stays, 0, 2))

    z_rows = pl.ds(pl.multiple_of(z * 32, 32), 32)
    for d in (1, 3, 2):
        send(zsend.at[z_at(d), 0:2], kv.at[blk, :, :, z_rows, :], "kvz", d, z_dev(d))
    kv[blk, :, :, z_rows, :] = zsend[z, 0:2]
    qd[:, :, z_rows, :] = zsend[z, 2:4]

    pick = lax.broadcasted_iota(jnp.int32, (64, 4), 0) // 16 == lax.broadcasted_iota(
        jnp.int32, (64, 4), 1)
    w_rows[...] = nn(pick.astype(bf16), w_bias[...]).astype(bf16)
    row_in = lax.rem(lax.broadcasted_iota(jnp.int32, (64, 128), 0), 16)

    def tile_step(i, acc):
        for u in range(4):
            jj = i * 4 + u
            tokens = jnp.concatenate([pair[q * 16 + jj] for q in range(4)], axis=0).astype(f32)
            hat, rstd, _ = norm(tokens)
            xhat[jj] = hat
            rstd_all[jj] = jnp.broadcast_to(rstd, (128, 128))
            normed = (hat * gain_v).astype(bf16)
            chosen = jnp.where(row_in == jj, w_rows[...].astype(f32), 0.0).astype(bf16)
            acc = acc + nt(chosen, normed)
        return acc

    tile_bias = lax.fori_loop(0, 4, tile_step, jnp.zeros((64, 128), f32))
    bsend[...] = tile_bias.astype(bf16).reshape(4, 16, 128)
    for e, d in ((0, 1), (0, 3), (0, 2), (1, 0), (1, 1), (1, 3), (1, 2)):
        send(bsend.at[z_at(d)], brecv.at[zhi, z], "bz", e * 4 + d, zz_dev(e, d))
    brecv[zhi, z] = bsend[z]
    for d in (1, 3, 2):
        send(zsend.at[z_at(d), 2:4], qd.at[:, :, z_rows, :], "qdz", d, z_dev(d))

    for d in (1, 2, 3):
        rows_d = pl.ds(pl.multiple_of(z_at(4 - d) * 32, 32), 32)
        arrived(kv.at[blk, :, :, rows_d, :], "kvz", d)
    send(kv.at[blk, 0], kv.at[blk, 0], "kva", 0, x_dev(1))
    send(kv.at[blk, 1], kv.at[blk, 1], "kva", 1, x_dev(3))
    send(kv.at[blk, 1], kv.at[blk, 1], "kva", 2, x_dev(1))
    send(kv.at[blk, 0], kv.at[blk, 0], "kva", 3, x_dev(3))
    send(kv.at[blk], kv.at[blk], "kvc", 0, core_dev)

    for e in range(2):
        for d in range(4):
            if (e, d) != (0, 0):
                arrived(brecv.at[lax.rem(zhi + e, 2), z_at(4 - d)], "bz", e * 4 + d)
    for e in range(2):
        outs = lane_swap([brecv[e, b].astype(f32) for b in range(4)])
        for q in range(4):
            grid[e, q * 16:(q + 1) * 16] = outs[q].astype(bf16)

    def half(c):
        return grid.at[:, pl.ds(pl.multiple_of(c * 32, 32), 32), :]

    turn(half(core), bias.at[blk, lax.rem(y, 2)], "bt", lax.rem(y, 2), by_column(core))
    send(half(other), bias.at[blk, lax.rem(y, 2)], "bt", 1, by_column(other), lax.rem(y, 2))

    k_minus, k_plus, k_two = x_at(3) * 2 + core, x_at(1) * 2 + core, x_at(2) * 2 + core
    arrived(kv.at[k_minus, 0], "kva", 0)
    send(kv.at[k_minus, 0], kv.at[k_minus, 0], "kvb", 0, x_dev(1))
    arrived(kv.at[k_plus, 1], "kva", 1)
    send(kv.at[k_plus, 1], kv.at[k_plus, 1], "kvb", 1, x_dev(3))

    arrived(bias.at[y, 0], "bt", 0)
    arrived(bias.at[y, 1], "bt", 1)
    for d in (2, 6, 1, 7):
        send(bias.at[y], bias.at[y], "ya", d, y_dev(d))

    arrived(kv.at[k_minus, 1], "kva", 2)
    send(kv.at[k_minus], kv.at[k_minus], "kvc", 1, core_dev)
    arrived(kv.at[k_plus, 0], "kva", 3)
    send(kv.at[k_plus], kv.at[k_plus], "kvc", 2, core_dev)

    for d in (1, 2, 3):
        rows_d = pl.ds(pl.multiple_of(z_at(4 - d) * 32, 32), 32)
        arrived(qd.at[:, :, rows_d, :], "qdz", d)
    for n in range(2):
        for g in range(2):
            qdt[n, g] = qd[n, g].astype(f32).T.astype(bf16)

    arrived(bias.at[y_at(6)], "ya", 2)
    send(bias.at[y_at(6)], bias.at[y_at(6)], "ya", 3, y_dev(1))
    send(bias.at[y_at(6), 0], bias.at[y_at(6), 0], "yb", 0, y_dev(2))
    arrived(bias.at[y_at(2)], "ya", 6)
    send(bias.at[y_at(2)], bias.at[y_at(2)], "ya", 5, y_dev(7))
    send(bias.at[y_at(2), 1], bias.at[y_at(2), 1], "yb", 1, y_dev(6))

    arrived(kv.at[k_two, 0], "kvb", 0)
    arrived(kv.at[k_two, 1], "kvb", 1)
    send(kv.at[k_two], kv.at[k_two], "kvc", 3, core_dev)

    arrived(bias.at[y_at(7)], "ya", 1)
    arrived(bias.at[y_at(1)], "ya", 7)
    arrived(bias.at[y_at(5)], "ya", 3)
    arrived(bias.at[y_at(3)], "ya", 5)
    arrived(bias.at[y_at(4), 0], "yb", 0)
    arrived(bias.at[y_at(4), 1], "yb", 1)
    for n, d in enumerate((0, 3, 1, 2)):
        arrived(kv.at[x_at(d) * 2 + other], "kvc", n)

    spot = lax.broadcasted_iota(jnp.int32, (1, 1024), 1)
    spot_c = (lax.div(spot, 256) * 8 + lax.rem(lax.div(spot, 32), 4) * 2
              + lax.rem(lax.div(spot, 128), 2))
    keep = spot_c * 32 + lax.rem(spot, 32) < length[0]
    for b in range(8):
        bias_f[:, b * 128:(b + 1) * 128] = bias[b].reshape(128, 128).astype(f32)
    dbias[...] = jnp.zeros_like(dbias)
    att[...] = jnp.zeros_like(att)
    dqkv[0] = jnp.zeros_like(dqkv[0])
    lanes = lane_block((128, 128))

    def cores_summed(g):
        arrived(dkv_c.at[g], "dkvc", g)
        for b in range(4):
            dkv_m[g, b] = (dkv_send[core, g, b].astype(f32) + dkv_c[g, b].astype(f32)).astype(bf16)
        send(dkv_m.at[g, x_at(2), 0], dkv_r.at[g, 0], "dr", g * 2, x_dev(1))
        send(dkv_m.at[g, x_at(2), 1], dkv_r.at[g, 1], "dr", g * 2 + 1, x_dev(3))
        send(dkv_m.at[g, x_at(1), 1], dkv_in.at[g, 0, 1], "df", g * 4, x_dev(1))
        send(dkv_m.at[g, x_at(3), 0], dkv_in.at[g, 1, 0], "df", g * 4 + 1, x_dev(3))

    for g in range(2):
        def attend(a, carry):
            own = lanes == a
            key = kv[:, 0, g].reshape(1024, 128)
            value = kv[:, 1, g].reshape(1024, 128)
            q_a = jnp.where(own, qd[0, g].astype(f32), 0.0).astype(bf16)
            do_f = jnp.where(own, qd[1, g].astype(f32), 0.0)
            do_a = do_f.astype(bf16)
            logits = jnp.where(keep, nt(q_a, key) + bias_f[...], NEG)
            top = jnp.max(logits, axis=-1, keepdims=True)
            expo = jnp.exp(logits - top)
            inv = 1.0 / jnp.sum(expo, axis=-1, keepdims=True)
            out = nn(expo.astype(bf16), value) * inv
            out = jnp.where(own, out, 0.0)
            att[g] = att[g] + out
            delta = jnp.sum(do_f * out, axis=-1, keepdims=True)
            shares = expo * inv
            grads = shares * (nt(do_a, value) - delta)
            for b in range(8):
                dbias[b] = dbias[b] + grads[:, b * 128:(b + 1) * 128]
            grads_b = grads.astype(bf16)
            dq = nn(grads_b, key) * (32 ** (-0.5))
            dqkv[0, g] = jnp.where(own, dq, dqkv[0, g].astype(f32)).astype(bf16)
            part = pl.ds(pl.multiple_of(a * 32, 32), 32)
            dk = nn(qdt[0, g, part, :], grads_b).astype(bf16)
            dv = nn(qdt[1, g, part, :], shares.astype(bf16)).astype(bf16)
            for b in range(8):
                dkv_send[b % 2, g, b // 2, 0, part, :] = dk[:, b * 128:(b + 1) * 128]
                dkv_send[b % 2, g, b // 2, 1, part, :] = dv[:, b * 128:(b + 1) * 128]
            return carry

        lax.fori_loop(0, 2, attend, 0)
        if g == 1:
            cores_summed(0)
        lax.fori_loop(2, 4, attend, 0)
        send(dkv_send.at[other, g], dkv_c.at[g], "dkvc", g, core_dev)

    for b in range(8):
        db_send[b] = dbias[b].astype(bf16)
    send(db_send.at[y_at(3)], db_r.at[0], "yr", 0, y_dev(1))
    send(db_send.at[y_at(5)], db_r.at[1], "yr", 1, y_dev(7))
    send(db_send.at[y_at(4), 0:64], db_rh.at[0], "yr", 2, y_dev(2))
    send(db_send.at[y_at(4), 64:128], db_rh.at[1], "yr", 3, y_dev(6))
    send(db_send.at[y_at(1)], db_y.at[0], "yd", 0, y_dev(1))
    send(db_send.at[y_at(7)], db_y.at[1], "yd", 1, y_dev(7))
    for d in (1, 3, 2):
        rows_d = pl.ds(pl.multiple_of(z_at(d) * 32, 32), 32)
        send(att.at[:, rows_d, :], o_in.at[z], "oz", d, z_dev(d))
        send(dqkv.at[0, :, rows_d, :], e_in.at[z, 0], "dqz", d, z_dev(d))
    o_in[z] = att[:, z_rows, :]
    e_in[z, 0] = dqkv[0, :, z_rows, :]

    cores_summed(1)

    arrived(db_r.at[0], "yr", 0)
    arrived(db_rh.at[0], "yr", 2)
    near = dbias[y_at(2)] + db_r[0].astype(f32)
    db_2[0, 0:64] = (near[0:64] + db_rh[0].astype(f32)).astype(bf16)
    db_2[0, 64:128] = near[64:128].astype(bf16)
    send(db_2.at[0], db_y.at[2], "yd", 2, y_dev(2))
    arrived(db_r.at[1], "yr", 1)
    arrived(db_rh.at[1], "yr", 3)
    near = dbias[y_at(6)] + db_r[1].astype(f32)
    db_2[1, 0:64] = near[0:64].astype(bf16)
    db_2[1, 64:128] = (near[64:128] + db_rh[1].astype(f32)).astype(bf16)
    send(db_2.at[1], db_y.at[3], "yd", 3, y_dev(6))

    for g in range(2):
        arrived(dkv_r.at[g, 0], "dr", g * 2)
        dkv_2[g, 0] = (dkv_m[g, x_at(1), 0].astype(f32) + dkv_r[g, 0].astype(f32)).astype(bf16)
        send(dkv_2.at[g, 0], dkv_in.at[g, 0, 0], "df", g * 4 + 2, x_dev(1))
        arrived(dkv_r.at[g, 1], "dr", g * 2 + 1)
        dkv_2[g, 1] = (dkv_m[g, x_at(3), 1].astype(f32) + dkv_r[g, 1].astype(f32)).astype(bf16)
        send(dkv_2.at[g, 1], dkv_in.at[g, 1, 1], "df", g * 4 + 3, x_dev(3))

    total = dbias[y]
    for n in range(4):
        arrived(db_y.at[n], "yd", n)
        total = total + db_y[n].astype(f32)
    db_s[...] = total.reshape(2, 64, 128)
    turn(db_s.at[core], db_t.at[core], "dt", core, by_row(core))
    send(db_s.at[other], db_t.at[core], "dt", 1, by_row(other), core)

    for g in range(2):
        arrived(dkv_in.at[g, 0, 1], "df", g * 4)
        arrived(dkv_in.at[g, 1, 0], "df", g * 4 + 1)
        arrived(dkv_in.at[g, 0, 0], "df", g * 4 + 2)
        arrived(dkv_in.at[g, 1, 1], "df", g * 4 + 3)
        for n in range(2):
            total = dkv_m[g, x, n].astype(f32) + (
                dkv_in[g, 0, n].astype(f32) + dkv_in[g, 1, n].astype(f32))
            dqkv[1 + n, g] = total.T.astype(bf16)
    for d in (1, 3, 2):
        rows_d = pl.ds(pl.multiple_of(z_at(d) * 32, 32), 32)
        send(dqkv.at[1:3, :, rows_d, :], e_in.at[z, 1:3], "dkvz", d, z_dev(d))
    e_in[z, 1:3] = dqkv[1:3, :, z_rows, :]

    arrived(db_t.at[0], "dt", 0)
    arrived(db_t.at[1], "dt", 1)
    for e in range(2):
        final = db_t[:, e * 32:(e + 1) * 32, :].reshape(64, 128)
        outs = lane_swap([final[q * 16:(q + 1) * 16] for q in range(4)])
        for b in range(4):
            db_out[e, b] = outs[b]
    for e, d in ((0, 1), (0, 3), (0, 2), (1, 0), (1, 1), (1, 3), (1, 2)):
        send(db_out.at[lax.rem(zhi + e, 2), z_at(d)], db_in.at[zhi, z], "dbz", e * 4 + d,
             zz_dev(e, d))
    db_in[zhi, z] = db_out[zhi, z]

    for d in (1, 2, 3):
        h_d = z_at(4 - d)
        arrived(o_in.at[h_d], "oz", d)
        arrived(e_in.at[h_d, 0], "dqz", d)
    gated = []
    pres = []
    for g in range(2):
        outs = lane_swap([o_in[h, g] for h in range(4)])
        for i in range(4):
            at = slice((g * 4 + i) * 32, (g * 4 + i + 1) * 32)
            gate_t, gg_t = gate_s[at], gg_s[at]
            gated.append((gate_t * outs[i]).astype(bf16))
            pres.append((gg_t * outs[i] * gate_t * (1.0 - gate_t)).astype(bf16))
    update[...] = nn(jnp.concatenate(gated, axis=0), w_out[...]).astype(bf16).reshape(8, 32, 128)
    for d in (1, 2, 3):
        arrived(e_in.at[z_at(4 - d), 1:3], "dkvz", d)
    sides = [jnp.concatenate(pres, axis=0)]
    for n in range(3):
        tiles = []
        for g in range(2):
            tiles += lane_swap([e_in[h, n, g].astype(f32) for h in range(4)])
        sides.append(jnp.concatenate(tiles, axis=0).astype(bf16))
    grad_window = (nt(sides[1], w_query[...]) + nt(sides[2], w_key[...])
                   + nt(sides[3], w_value[...]) + nt(sides[0], w_gate[...]))
    gw[0:8] = grad_window.reshape(8, 32, 128)
    gw[8:16] = jnp.zeros((8, 32, 128), f32)

    for e in range(2):
        for d in range(4):
            if (e, d) != (0, 0):
                arrived(db_in.at[lax.rem(zhi + e, 2), z_at(4 - d)], "dbz", e * 4 + d)
    flat = (db_in[0] + db_in[1]).reshape(64, 128).T
    high = flat.astype(bf16)
    rest = flat - high.astype(f32)
    mid = rest.astype(bf16)
    low = (rest - mid.astype(f32)).astype(bf16)

    def final_step(i, carry):
        for u in range(2):
            jj = i * 2 + u
            chosen = jnp.where(row_in == jj, w_rows[...].astype(f32), 0.0).astype(bf16)
            grad = nn(high, chosen) + (nn(mid, chosen) + nn(low, chosen))
            grad = jnp.concatenate([grad[0:32] + gw[jj], grad[32:]], axis=0) * gain_v
            hat = xhat[jj]
            first = jnp.mean(grad, axis=-1, keepdims=True)
            second = jnp.mean(grad * hat, axis=-1, keepdims=True)
            result = rstd_all[jj] * (grad - first - hat * second)
            for q in range(4):
                pair_grad[q * 16 + jj] = result[q * 32:(q + 1) * 32]
        return carry

    lax.fori_loop(0, 8, final_step, 0)

    for copy in sent:
        copy.wait_send()

    @pl.when(jnp.logical_not(stays))
    def _():
        for copy in turned:
            copy.wait_send()


def body(pair, length, ln_gain, w_query, w_key, w_value, w_gate, w_bias, w_out, out_grad):
    vmem = pl.BlockSpec(memory_space=pltpu.VMEM)
    hbm = pl.BlockSpec(memory_space=pltpu.HBM)
    smem = pl.BlockSpec(memory_space=pltpu.SMEM)

    scratch = [
        pltpu.VMEM(pair.shape, bf16),
        *[pltpu.VMEM((128, 128), bf16) for _ in range(5)],
        pltpu.VMEM(out_grad.shape, bf16),
        pltpu.SemaphoreType.DMA((7,)),
        pltpu.VMEM((16, 128, 128), f32),
        pltpu.VMEM((16, 128, 128), f32),
        pltpu.VMEM((64, 128), bf16),
        pltpu.VMEM((256, 128), f32),
        pltpu.VMEM((256, 128), f32),
        pltpu.VMEM((4, 4, 2, 32, 128), bf16),
        pltpu.VMEM((8, 2, 2, 128, 128), bf16),
        pltpu.VMEM((2, 2, 128, 128), bf16),
        pltpu.VMEM((2, 2, 128, 128), bf16),
        pltpu.VMEM((4, 16, 128), bf16),
        pltpu.VMEM((2, 4, 16, 128), bf16),
        pltpu.VMEM((2, 64, 128), bf16),
        pltpu.VMEM((8, 2, 2, 32, 128), bf16),
        pltpu.VMEM((128, 1024), f32),
        pltpu.VMEM((8, 128, 128), f32),
        pltpu.VMEM((2, 128, 128), f32),
        pltpu.VMEM((3, 2, 128, 128), bf16),
        pltpu.VMEM((8, 128, 128), bf16),
        pltpu.VMEM((2, 128, 128), bf16),
        pltpu.VMEM((2, 64, 128), bf16),
        pltpu.VMEM((2, 128, 128), bf16),
        pltpu.VMEM((4, 128, 128), bf16),
        pltpu.VMEM((2, 64, 128), f32),
        pltpu.VMEM((2, 64, 128), f32),
        pltpu.VMEM((2, 4, 16, 128), f32),
        pltpu.VMEM((2, 4, 16, 128), f32),
        pltpu.VMEM((2, 2, 4, 2, 128, 128), bf16),
        pltpu.VMEM((2, 4, 2, 128, 128), bf16),
        pltpu.VMEM((2, 4, 2, 128, 128), bf16),
        pltpu.VMEM((2, 2, 128, 128), bf16),
        pltpu.VMEM((2, 2, 128, 128), bf16),
        pltpu.VMEM((2, 2, 2, 128, 128), bf16),
        pltpu.VMEM((4, 3, 2, 32, 128), bf16),
        pltpu.VMEM((4, 2, 32, 128), f32),
        pltpu.VMEM((16, 32, 128), f32),
    ]
    for _, n in COPIES:
        scratch += [pltpu.SemaphoreType.DMA((n,)), pltpu.SemaphoreType.DMA((n,))]
    call = pl.pallas_call(
        kernel,
        out_shape=(
            jax.ShapeDtypeStruct(out_grad.shape, bf16),
            jax.ShapeDtypeStruct(pair.shape, f32),
        ),
        in_specs=[hbm, smem, vmem, hbm, hbm, hbm, hbm, vmem, hbm, hbm],
        out_specs=(vmem, vmem),
        scratch_shapes=scratch,
        compiler_params=pltpu.CompilerParams(
            collective_id=0, has_side_effects=True, vmem_limit_bytes=63 * 1024 * 1024
        ),
    )
    return call(
        pair, length, ln_gain.reshape(1, 128), w_query, w_key, w_value, w_gate, w_bias.T, w_out,
        out_grad,
    )


def solution(mesh):
    tiled = P("rows", "cols", None)
    placed = (tiled, P(), P(), P(), P(), P(), P(), P(), P(), tiled)
    return jax.shard_map(
        body, mesh=mesh, in_specs=placed, out_specs=(tiled, tiled), check_vma=False
    )
```

```python
import jax
import jax.numpy as jnp
from jax import lax
from jax.experimental import pallas as pl
from jax.experimental.pallas import tpu as pltpu
from jax.sharding import PartitionSpec as P

EPS = 1e-05
NEG = -1000000000.0
MESH = pl.DeviceIdType.MESH
f32 = jnp.float32
bf16 = jnp.bfloat16
COPIES = (
    ("kvz", 4), ("qdz", 4), ("bt", 16), ("kvx", 4), ("kvc", 4), ("ya", 8), ("dkvc", 2), ("dr", 8),
    ("yr", 8), ("dt", 16), ("oz", 4), ("dqz", 4), ("dkvz", 4),
)

AROUND = ((0, 0), (0, 1), (0, 3), (0, 2), (1, 0), (1, 1), (1, 3), (1, 2))


def nn(left, right):
    return lax.dot_general(left, right, (((1,), (0,)), ((), ())), preferred_element_type=f32)


def nt(left, right):
    return lax.dot_general(left, right, (((1,), (1,)), ((), ())), preferred_element_type=f32)


def lane_block(shape):
    return lax.shift_right_logical(lax.broadcasted_iota(jnp.int32, shape, len(shape) - 1), 5)


def lane_swap(tiles):
    block = lane_block(tiles[0].shape)
    outs = []
    for i in range(4):
        acc = None
        for b in range(4):
            shift = (32 * (b - i)) % 128
            moved = tiles[b] if shift == 0 else pltpu.roll(tiles[b], shift, 1)
            acc = moved if acc is None else jnp.where(block == b, moved, acc)
        outs.append(acc)
    return outs


def remote(src, dst, send_sem, recv_sem, device):
    return pltpu.make_async_remote_copy(
        src_ref=src, dst_ref=dst, send_sem=send_sem, recv_sem=recv_sem,
        device_id=device, device_id_type=MESH,
    )


def kernel(
    pair_h, length, gain, w_query_h, w_key_h, w_value_h, w_gate_h, w_bias, w_out_h, out_grad_h,
    update, pair_grad,
    pair, w_query, w_key, w_value, w_gate, w_out, out_grad, load_sem, xhat, rstd_all, w_rows, gate_s, gg_s, zsend, kv, qd, qdt, bsend, brecv, bias, bias_f,
    dbias, att, dqkv, db_send, db_y, db_out, db_in, dkv_send, dkv_c, dkv_m, dkv_in,
    e_in, o_in, gw,
    *sems,
):
    sem = {name: sems[2 * n:2 * n + 2] for n, (name, _) in enumerate(COPIES)}
    row = lax.axis_index("rows")
    col = lax.axis_index("cols")
    y, zhi = lax.div(row, 2), lax.rem(row, 2)
    x, z, core = lax.div(col, 8), lax.rem(lax.div(col, 2), 4), lax.rem(col, 2)
    blk = x * 2 + core
    other = 1 - core

    def device(row_, x_, z_, core_):
        return {"rows": row_, "cols": x_ * 8 + z_ * 2 + core_}

    def z_at(d):
        return lax.rem(z + d, 4)

    def z_dev(d):
        return device(row, x, z_at(d), core)

    def x_at(d):
        return lax.rem(x + d, 4)

    def x_dev(d):
        return device(row, x_at(d), z, core)

    def y_at(d):
        return lax.rem(y + d, 8)

    def y_dev(d):
        return device(y_at(d) * 2 + zhi, x, z, core)

    def by_column(e, d, c):
        return device(blk * 2 + lax.rem(zhi + e, 2), lax.div(y, 2), z_at(d), c)

    def by_row(e, d, s):
        return device(
            (x * 2 + s) * 2 + lax.rem(zhi + e, 2), lax.div(y, 2), z_at(d), lax.rem(y, 2))

    core_dev = device(row, x, z, other)
    stays = blk == y

    sent = []
    turned = []

    def send(src, dst, name, n, dev, at=None):
        copy = remote(src, dst, sem[name][0].at[n], sem[name][1].at[n if at is None else at], dev)
        copy.start()
        sent.append(copy)

    def turn_own(src, dst, name, at, dev):
        away = remote(src, dst, sem[name][0].at[0], sem[name][1].at[at], dev)
        here = pltpu.make_async_copy(src, dst, sem[name][1].at[at])

        @pl.when(stays)
        def _():
            here.start()

        @pl.when(jnp.logical_not(stays))
        def _():
            away.start()

        turned.append(away)

    def arrived(slot, name, n):
        remote(slot, slot, sem[name][0].at[n], sem[name][1].at[n], core_dev).wait_recv()

    loads = [
        pltpu.make_async_copy(src, dst, load_sem.at[n])
        for n, (src, dst) in enumerate((
            (pair_h, pair), (w_query_h, w_query), (w_key_h, w_key), (w_value_h, w_value),
            (w_gate_h, w_gate), (w_out_h, w_out), (out_grad_h, out_grad)))
    ]
    for copy in loads:
        copy.start()

    barrier = pltpu.get_barrier_semaphore()
    turns = [(e, d, other) for e in range(2) for d in range(4)]
    turns += [(e, d, core) for e in range(2) for d in range(4) if (e, d) != (0, 0)]
    partners = [z_dev(d) for d in (1, 2, 3)] + [core_dev] + [x_dev(d) for d in (1, 2, 3)]
    partners += [y_dev(d) for d in range(1, 8)]
    partners += [by_column(*turn) for turn in turns] + [by_row(*turn) for turn in turns]

    def greet(dev):
        pl.semaphore_signal(barrier, inc=1, device_id=dev, device_id_type=MESH)

    for dev in partners:
        greet(dev)

    @pl.when(jnp.logical_not(stays))
    def _():
        greet(by_column(0, 0, core))
        greet(by_row(0, 0, core))

    gain_v = gain[...]
    for copy in loads:
        copy.wait()

    def norm(values):
        average = jnp.mean(values, axis=-1, keepdims=True)
        centred = values - average
        variance = jnp.mean(centred * centred, axis=-1, keepdims=True)
        rstd = lax.rsqrt(variance + EPS)
        return centred * rstd, rstd, centred

    win = pair[0:8].reshape(256, 128).astype(f32)
    hat, _, _ = norm(win)
    window = (hat * gain_v).astype(bf16)
    query = (nn(window, w_query[...]) * (32 ** (-0.5))).astype(bf16).astype(f32)
    keys = nn(window, w_key[...]).astype(bf16).astype(f32)
    vals = nn(window, w_value[...]).astype(bf16).astype(f32)
    gate = jax.nn.sigmoid(nn(window, w_gate[...])).astype(bf16).astype(f32)
    gg = nt(out_grad[...].reshape(256, 128), w_out[...])
    ga = (gg * gate).astype(bf16).astype(f32)
    gate_s[...] = gate
    gg_s[...] = gg
    for n, array in enumerate((keys, vals, query, ga)):
        for g in range(2):
            outs = lane_swap([array[(g * 4 + b) * 32:(g * 4 + b + 1) * 32] for b in range(4)])
            for h in range(4):
                zsend[h, n, g] = outs[h].astype(bf16)

    pl.semaphore_wait(barrier, len(partners) + jnp.where(stays, 0, 2))

    z_rows = pl.ds(pl.multiple_of(z * 32, 32), 32)
    for d in (1, 3, 2):
        send(zsend.at[z_at(d), 0:2], kv.at[blk, :, :, z_rows, :], "kvz", d, z_dev(d))
    kv[blk, :, :, z_rows, :] = zsend[z, 0:2]
    qd[:, :, z_rows, :] = zsend[z, 2:4]

    pick = lax.broadcasted_iota(jnp.int32, (64, 4), 0) // 16 == lax.broadcasted_iota(
        jnp.int32, (64, 4), 1)
    w_rows[...] = nn(pick.astype(bf16), w_bias[...]).astype(bf16)
    row_in = lax.rem(lax.broadcasted_iota(jnp.int32, (64, 128), 0), 16)

    def tile_step(i, acc):
        for u in range(4):
            jj = i * 4 + u
            tokens = jnp.concatenate([pair[q * 16 + jj] for q in range(4)], axis=0).astype(f32)
            hat, rstd, _ = norm(tokens)
            xhat[jj] = hat
            rstd_all[jj] = jnp.broadcast_to(rstd, (128, 128))
            normed = (hat * gain_v).astype(bf16)
            chosen = jnp.where(row_in == jj, w_rows[...].astype(f32), 0.0).astype(bf16)
            acc = acc + nt(chosen, normed)
        return acc

    tile_bias = lax.fori_loop(0, 4, tile_step, jnp.zeros((64, 128), f32))
    bsend[...] = tile_bias.astype(bf16).reshape(4, 16, 128)
    odd = lax.rem(y, 2)
    turn_own(bsend.at[z], brecv.at[odd, zhi, z], "bt", odd * 8, by_column(0, 0, core))
    for n, c in enumerate((core, other)):
        for e, d in AROUND:
            if (n, e, d) != (0, 0, 0):
                send(bsend.at[z_at(d)], brecv.at[odd, zhi, z], "bt", n * 8 + e * 4 + d,
                     by_column(e, d, c), odd * 8 + e * 4 + d)
    for d in (1, 3, 2):
        send(zsend.at[z_at(d), 2:4], qd.at[:, :, z_rows, :], "qdz", d, z_dev(d))

    for d in (1, 2, 3):
        rows_d = pl.ds(pl.multiple_of(z_at(4 - d) * 32, 32), 32)
        arrived(kv.at[blk, :, :, rows_d, :], "kvz", d)
    for d in (1, 3, 2):
        send(kv.at[blk], kv.at[blk], "kvx", d, x_dev(d))
    send(kv.at[blk], kv.at[blk], "kvc", 0, core_dev)

    for n in range(2):
        for e, d in AROUND:
            arrived(brecv.at[n, lax.rem(zhi + e, 2), z_at(4 - d)], "bt", n * 8 + e * 4 + d)
    for n in range(2):
        for e in range(2):
            outs = lane_swap([brecv[n, e, b].astype(f32) for b in range(4)])
            bias[y, n, e, 0:16] = jnp.where(core == 0, outs[0], outs[2]).astype(bf16)
            bias[y, n, e, 16:32] = jnp.where(core == 0, outs[1], outs[3]).astype(bf16)
    for d in (4, 3, 5, 2, 6, 1, 7):
        send(bias.at[y], bias.at[y], "ya", d, y_dev(d))

    for d in (1, 2, 3):
        rows_d = pl.ds(pl.multiple_of(z_at(4 - d) * 32, 32), 32)
        arrived(qd.at[:, :, rows_d, :], "qdz", d)
    for n in range(2):
        for g in range(2):
            qdt[n, g] = qd[n, g].astype(f32).T.astype(bf16)

    for d in (1, 3, 2):
        k_d = x_at(4 - d) * 2 + core
        arrived(kv.at[k_d], "kvx", d)
        send(kv.at[k_d], kv.at[k_d], "kvc", d, core_dev)
    for d in (0, 1, 3, 2):
        arrived(kv.at[x_at(4 - d) * 2 + other], "kvc", d)

    for d in range(1, 8):
        arrived(bias.at[y_at(8 - d)], "ya", d)

    spot = lax.broadcasted_iota(jnp.int32, (1, 1024), 1)
    spot_c = (lax.div(spot, 256) * 8 + lax.rem(lax.div(spot, 32), 4) * 2
              + lax.rem(lax.div(spot, 128), 2))
    keep = spot_c * 32 + lax.rem(spot, 32) < length[0]
    for b in range(8):
        bias_f[:, b * 128:(b + 1) * 128] = bias[b].reshape(128, 128).astype(f32)
    dbias[...] = jnp.zeros_like(dbias)
    att[...] = jnp.zeros_like(att)
    dqkv[0] = jnp.zeros_like(dqkv[0])
    lanes = lane_block((128, 128))

    def cores_summed(g):
        arrived(dkv_c.at[g], "dkvc", g)
        for b in range(4):
            dkv_m[g, b] = (dkv_send[core, g, b].astype(f32) + dkv_c[g, b].astype(f32)).astype(bf16)
        for d in (1, 3, 2):
            send(dkv_m.at[g, x_at(d)], dkv_in.at[g, d], "dr", g * 4 + d, x_dev(d))

    for g in range(2):
        def attend(a, carry):
            own = lanes == a
            key = kv[:, 0, g].reshape(1024, 128)
            value = kv[:, 1, g].reshape(1024, 128)
            q_a = jnp.where(own, qd[0, g].astype(f32), 0.0).astype(bf16)
            do_f = jnp.where(own, qd[1, g].astype(f32), 0.0)
            do_a = do_f.astype(bf16)
            logits = jnp.where(keep, nt(q_a, key) + bias_f[...], NEG)
            top = jnp.max(logits, axis=-1, keepdims=True)
            expo = jnp.exp(logits - top)
            inv = 1.0 / jnp.sum(expo, axis=-1, keepdims=True)
            out = nn(expo.astype(bf16), value) * inv
            out = jnp.where(own, out, 0.0)
            att[g] = att[g] + out
            delta = jnp.sum(do_f * out, axis=-1, keepdims=True)
            shares = expo * inv
            grads = shares * (nt(do_a, value) - delta)
            for b in range(8):
                dbias[b] = dbias[b] + grads[:, b * 128:(b + 1) * 128]
            grads_b = grads.astype(bf16)
            dq = nn(grads_b, key) * (32 ** (-0.5))
            dqkv[0, g] = jnp.where(own, dq, dqkv[0, g].astype(f32)).astype(bf16)
            part = pl.ds(pl.multiple_of(a * 32, 32), 32)
            dk = nn(qdt[0, g, part, :], grads_b).astype(bf16)
            dv = nn(qdt[1, g, part, :], shares.astype(bf16)).astype(bf16)
            for b in range(8):
                dkv_send[b % 2, g, b // 2, 0, part, :] = dk[:, b * 128:(b + 1) * 128]
                dkv_send[b % 2, g, b // 2, 1, part, :] = dv[:, b * 128:(b + 1) * 128]
            return carry

        lax.fori_loop(0, 2, attend, 0)
        if g == 1:
            cores_summed(0)
        lax.fori_loop(2, 4, attend, 0)
        send(dkv_send.at[other, g], dkv_c.at[g], "dkvc", g, core_dev)

    for b in range(8):
        db_send[b] = dbias[b].astype(bf16)
    for d in (4, 3, 5, 2, 6, 1, 7):
        send(db_send.at[y_at(d)], db_y.at[d], "yr", d, y_dev(d))
    for d in (1, 3, 2):
        rows_d = pl.ds(pl.multiple_of(z_at(d) * 32, 32), 32)
        send(att.at[:, rows_d, :], o_in.at[z], "oz", d, z_dev(d))
        send(dqkv.at[0, :, rows_d, :], e_in.at[z, 0], "dqz", d, z_dev(d))
    o_in[z] = att[:, z_rows, :]
    e_in[z, 0] = dqkv[0, :, z_rows, :]

    cores_summed(1)

    total = dbias[y]
    for d in range(1, 8):
        arrived(db_y.at[d], "yr", d)
        total = total + db_y[d].astype(f32)
    total = total.reshape(2, 2, 2, 16, 128)
    for n in range(2):
        for e in range(2):
            tiles = [jnp.where(core == c, total[n, e, i], 0.0) for c in range(2) for i in range(2)]
            outs = lane_swap(tiles)
            for b in range(4):
                db_out[n, e, b] = outs[b]
    turn_own(db_out.at[core, zhi, z], db_in.at[core, zhi, z], "dt", core * 8, by_row(0, 0, core))
    for n, c in enumerate((core, other)):
        for e, d in AROUND:
            if (n, e, d) != (0, 0, 0):
                send(db_out.at[c, lax.rem(zhi + e, 2), z_at(d)], db_in.at[core, zhi, z], "dt",
                     n * 8 + e * 4 + d, by_row(e, d, c), core * 8 + e * 4 + d)

    for g in range(2):
        for d in (1, 3, 2):
            arrived(dkv_in.at[g, d], "dr", g * 4 + d)
        for n in range(2):
            total = dkv_m[g, x, n].astype(f32)
            for d in (1, 2, 3):
                total = total + dkv_in[g, d, n].astype(f32)
            dqkv[1 + n, g] = total.T.astype(bf16)
    for d in (1, 3, 2):
        rows_d = pl.ds(pl.multiple_of(z_at(d) * 32, 32), 32)
        send(dqkv.at[1:3, :, rows_d, :], e_in.at[z, 1:3], "dkvz", d, z_dev(d))
    e_in[z, 1:3] = dqkv[1:3, :, z_rows, :]

    for d in (1, 2, 3):
        h_d = z_at(4 - d)
        arrived(o_in.at[h_d], "oz", d)
        arrived(e_in.at[h_d, 0], "dqz", d)
    gated = []
    pres = []
    for g in range(2):
        outs = lane_swap([o_in[h, g] for h in range(4)])
        for i in range(4):
            at = slice((g * 4 + i) * 32, (g * 4 + i + 1) * 32)
            gate_t, gg_t = gate_s[at], gg_s[at]
            gated.append((gate_t * outs[i]).astype(bf16))
            pres.append((gg_t * outs[i] * gate_t * (1.0 - gate_t)).astype(bf16))
    update[...] = nn(jnp.concatenate(gated, axis=0), w_out[...]).astype(bf16).reshape(8, 32, 128)
    for d in (1, 2, 3):
        arrived(e_in.at[z_at(4 - d), 1:3], "dkvz", d)
    sides = [jnp.concatenate(pres, axis=0)]
    for n in range(3):
        tiles = []
        for g in range(2):
            tiles += lane_swap([e_in[h, n, g].astype(f32) for h in range(4)])
        sides.append(jnp.concatenate(tiles, axis=0).astype(bf16))
    grad_window = (nt(sides[1], w_query[...]) + nt(sides[2], w_key[...])
                   + nt(sides[3], w_value[...]) + nt(sides[0], w_gate[...]))
    gw[0:8] = grad_window.reshape(8, 32, 128)
    gw[8:16] = jnp.zeros((8, 32, 128), f32)

    for n in range(2):
        for e, d in AROUND:
            arrived(db_in.at[n, lax.rem(zhi + e, 2), z_at(4 - d)], "dt", n * 8 + e * 4 + d)
    flat = ((db_in[0, 0] + db_in[0, 1]) + (db_in[1, 0] + db_in[1, 1])).reshape(64, 128).T
    high = flat.astype(bf16)
    rest = flat - high.astype(f32)
    mid = rest.astype(bf16)
    low = (rest - mid.astype(f32)).astype(bf16)

    def final_step(i, carry):
        for u in range(2):
            jj = i * 2 + u
            chosen = jnp.where(row_in == jj, w_rows[...].astype(f32), 0.0).astype(bf16)
            grad = nn(high, chosen) + (nn(mid, chosen) + nn(low, chosen))
            grad = jnp.concatenate([grad[0:32] + gw[jj], grad[32:]], axis=0) * gain_v
            hat = xhat[jj]
            first = jnp.mean(grad, axis=-1, keepdims=True)
            second = jnp.mean(grad * hat, axis=-1, keepdims=True)
            result = rstd_all[jj] * (grad - first - hat * second)
            for q in range(4):
                pair_grad[q * 16 + jj] = result[q * 32:(q + 1) * 32]
        return carry

    lax.fori_loop(0, 8, final_step, 0)

    for copy in sent:
        copy.wait_send()

    @pl.when(jnp.logical_not(stays))
    def _():
        for copy in turned:
            copy.wait_send()


def body(pair, length, ln_gain, w_query, w_key, w_value, w_gate, w_bias, w_out, out_grad):
    vmem = pl.BlockSpec(memory_space=pltpu.VMEM)
    hbm = pl.BlockSpec(memory_space=pltpu.HBM)
    smem = pl.BlockSpec(memory_space=pltpu.SMEM)

    scratch = [
        pltpu.VMEM(pair.shape, bf16),
        *[pltpu.VMEM((128, 128), bf16) for _ in range(5)],
        pltpu.VMEM(out_grad.shape, bf16),
        pltpu.SemaphoreType.DMA((7,)),
        pltpu.VMEM((16, 128, 128), f32),
        pltpu.VMEM((16, 128, 128), f32),
        pltpu.VMEM((64, 128), bf16),
        pltpu.VMEM((256, 128), f32),
        pltpu.VMEM((256, 128), f32),
        pltpu.VMEM((4, 4, 2, 32, 128), bf16),
        pltpu.VMEM((8, 2, 2, 128, 128), bf16),
        pltpu.VMEM((2, 2, 128, 128), bf16),
        pltpu.VMEM((2, 2, 128, 128), bf16),
        pltpu.VMEM((4, 16, 128), bf16),
        pltpu.VMEM((2, 2, 4, 16, 128), bf16),
        pltpu.VMEM((8, 2, 2, 32, 128), bf16),
        pltpu.VMEM((128, 1024), f32),
        pltpu.VMEM((8, 128, 128), f32),
        pltpu.VMEM((2, 128, 128), f32),
        pltpu.VMEM((3, 2, 128, 128), bf16),
        pltpu.VMEM((8, 128, 128), bf16),
        pltpu.VMEM((8, 128, 128), bf16),
        pltpu.VMEM((2, 2, 4, 16, 128), f32),
        pltpu.VMEM((2, 2, 4, 16, 128), f32),
        pltpu.VMEM((2, 2, 4, 2, 128, 128), bf16),
        pltpu.VMEM((2, 4, 2, 128, 128), bf16),
        pltpu.VMEM((2, 4, 2, 128, 128), bf16),
        pltpu.VMEM((2, 4, 2, 128, 128), bf16),
        pltpu.VMEM((4, 3, 2, 32, 128), bf16),
        pltpu.VMEM((4, 2, 32, 128), f32),
        pltpu.VMEM((16, 32, 128), f32),
    ]
    for _, n in COPIES:
        scratch += [pltpu.SemaphoreType.DMA((n,)), pltpu.SemaphoreType.DMA((n,))]
    call = pl.pallas_call(
        kernel,
        out_shape=(
            jax.ShapeDtypeStruct(out_grad.shape, bf16),
            jax.ShapeDtypeStruct(pair.shape, f32),
        ),
        in_specs=[hbm, smem, vmem, hbm, hbm, hbm, hbm, vmem, hbm, hbm],
        out_specs=(vmem, vmem),
        scratch_shapes=scratch,
        compiler_params=pltpu.CompilerParams(
            collective_id=0, has_side_effects=True, vmem_limit_bytes=63 * 1024 * 1024
        ),
    )
    return call(
        pair, length, ln_gain.reshape(1, 128), w_query, w_key, w_value, w_gate, w_bias.T, w_out,
        out_grad,
    )


def solution(mesh):
    tiled = P("rows", "cols", None)
    placed = (tiled, P(), P(), P(), P(), P(), P(), P(), P(), tiled)
    return jax.shard_map(
        body, mesh=mesh, in_specs=placed, out_specs=(tiled, tiled), check_vma=False
    )
```

```python
import jax
import jax.numpy as jnp
from jax import lax
from jax.experimental import pallas as pl
from jax.experimental.pallas import tpu as pltpu
from jax.sharding import PartitionSpec as P

EPS = 1e-05
NEG = -1000000000.0
MESH = pl.DeviceIdType.MESH
f32 = jnp.float32
bf16 = jnp.bfloat16
COPIES = (
    ("kvz", 4), ("qdz", 4), ("bt", 16), ("kvx", 4), ("kvc", 4), ("ya", 8), ("dkvc", 2), ("dr", 8),
    ("yr", 8), ("dt", 2), ("dbz", 8), ("oz", 4), ("dqz", 4), ("dkvz", 4),
)

AROUND = ((0, 0), (0, 1), (0, 3), (0, 2), (1, 0), (1, 1), (1, 3), (1, 2))


def nn(left, right):
    return lax.dot_general(left, right, (((1,), (0,)), ((), ())), preferred_element_type=f32)


def nt(left, right):
    return lax.dot_general(left, right, (((1,), (1,)), ((), ())), preferred_element_type=f32)


def lane_block(shape):
    return lax.shift_right_logical(lax.broadcasted_iota(jnp.int32, shape, len(shape) - 1), 5)


def lane_swap(tiles):
    block = lane_block(tiles[0].shape)
    outs = []
    for i in range(4):
        acc = None
        for b in range(4):
            shift = (32 * (b - i)) % 128
            moved = tiles[b] if shift == 0 else pltpu.roll(tiles[b], shift, 1)
            acc = moved if acc is None else jnp.where(block == b, moved, acc)
        outs.append(acc)
    return outs


def remote(src, dst, send_sem, recv_sem, device):
    return pltpu.make_async_remote_copy(
        src_ref=src, dst_ref=dst, send_sem=send_sem, recv_sem=recv_sem,
        device_id=device, device_id_type=MESH,
    )


def kernel(
    pair_h, length, gain, w_query_h, w_key_h, w_value_h, w_gate_h, w_bias, w_out_h, out_grad_h,
    update, pair_grad,
    pair, w_query, w_key, w_value, w_gate, w_out, out_grad, load_sem, xhat, rstd_all, w_rows, gate_s, gg_s, zsend, kv, qd, qdt, bsend, brecv, bias, bias_f,
    dbias, att, dqkv, db_send, db_y, db_s, db_t, db_out, db_in, dkv_send, dkv_c, dkv_m, dkv_in,
    e_in, o_in, gw,
    *sems,
):
    sem = {name: sems[2 * n:2 * n + 2] for n, (name, _) in enumerate(COPIES)}
    row = lax.axis_index("rows")
    col = lax.axis_index("cols")
    y, zhi = lax.div(row, 2), lax.rem(row, 2)
    x, z, core = lax.div(col, 8), lax.rem(lax.div(col, 2), 4), lax.rem(col, 2)
    blk = x * 2 + core
    other = 1 - core

    def device(row_, x_, z_, core_):
        return {"rows": row_, "cols": x_ * 8 + z_ * 2 + core_}

    def z_at(d):
        return lax.rem(z + d, 4)

    def z_dev(d):
        return device(row, x, z_at(d), core)

    def x_at(d):
        return lax.rem(x + d, 4)

    def x_dev(d):
        return device(row, x_at(d), z, core)

    def y_at(d):
        return lax.rem(y + d, 8)

    def y_dev(d):
        return device(y_at(d) * 2 + zhi, x, z, core)

    def zz_dev(e, d):
        return device(y * 2 + lax.rem(zhi + e, 2), x, z_at(d), core)

    def by_column(e, d, c):
        return device(blk * 2 + lax.rem(zhi + e, 2), lax.div(y, 2), z_at(d), c)

    def by_row_all(e, d, s):
        return device(
            (x * 2 + s) * 2 + lax.rem(zhi + e, 2), lax.div(y, 2), z_at(d), lax.rem(y, 2))

    def by_row(s):
        return device((x * 2 + s) * 2 + zhi, lax.div(y, 2), z, lax.rem(y, 2))

    core_dev = device(row, x, z, other)
    stays = blk == y

    sent = []
    turned = []

    def send(src, dst, name, n, dev, at=None):
        copy = remote(src, dst, sem[name][0].at[n], sem[name][1].at[n if at is None else at], dev)
        copy.start()
        sent.append(copy)

    def turn_own(src, dst, name, at, dev):
        away = remote(src, dst, sem[name][0].at[0], sem[name][1].at[at], dev)
        here = pltpu.make_async_copy(src, dst, sem[name][1].at[at])

        @pl.when(stays)
        def _():
            here.start()

        @pl.when(jnp.logical_not(stays))
        def _():
            away.start()

        turned.append(away)

    def arrived(slot, name, n):
        remote(slot, slot, sem[name][0].at[n], sem[name][1].at[n], core_dev).wait_recv()

    loads = [
        pltpu.make_async_copy(src, dst, load_sem.at[n])
        for n, (src, dst) in enumerate((
            (pair_h, pair), (w_query_h, w_query), (w_key_h, w_key), (w_value_h, w_value),
            (w_gate_h, w_gate), (w_out_h, w_out), (out_grad_h, out_grad)))
    ]
    for copy in loads:
        copy.start()

    barrier = pltpu.get_barrier_semaphore()
    turns = [(e, d, other) for e in range(2) for d in range(4)]
    turns += [(e, d, core) for e in range(2) for d in range(4) if (e, d) != (0, 0)]
    partners = [zz_dev(e, d) for e, d in AROUND[1:]]
    partners += [core_dev] + [x_dev(d) for d in (1, 2, 3)] + [y_dev(d) for d in range(1, 8)]
    partners += [by_row_all(*turn) for turn in turns] + [by_column(0, 0, other)]

    def greet(dev):
        pl.semaphore_signal(barrier, inc=1, device_id=dev, device_id_type=MESH)

    for dev in partners:
        greet(dev)

    @pl.when(jnp.logical_not(stays))
    def _():
        greet(by_column(0, 0, core))
        greet(by_row(core))

    gain_v = gain[...]
    for copy in loads:
        copy.wait()

    def norm(values):
        average = jnp.mean(values, axis=-1, keepdims=True)
        centred = values - average
        variance = jnp.mean(centred * centred, axis=-1, keepdims=True)
        rstd = lax.rsqrt(variance + EPS)
        return centred * rstd, rstd, centred

    win = pair[0:8].reshape(256, 128).astype(f32)
    hat, _, _ = norm(win)
    window = (hat * gain_v).astype(bf16)
    query = (nn(window, w_query[...]) * (32 ** (-0.5))).astype(bf16).astype(f32)
    keys = nn(window, w_key[...]).astype(bf16).astype(f32)
    vals = nn(window, w_value[...]).astype(bf16).astype(f32)
    gate = jax.nn.sigmoid(nn(window, w_gate[...])).astype(bf16).astype(f32)
    gg = nt(out_grad[...].reshape(256, 128), w_out[...])
    ga = (gg * gate).astype(bf16).astype(f32)
    gate_s[...] = gate
    gg_s[...] = gg
    for n, array in enumerate((keys, vals, query, ga)):
        for g in range(2):
            outs = lane_swap([array[(g * 4 + b) * 32:(g * 4 + b + 1) * 32] for b in range(4)])
            for h in range(4):
                zsend[h, n, g] = outs[h].astype(bf16)

    pl.semaphore_wait(barrier, len(partners) + jnp.where(stays, 0, 2))

    z_rows = pl.ds(pl.multiple_of(z * 32, 32), 32)
    for d in (1, 3, 2):
        send(zsend.at[z_at(d), 0:2], kv.at[blk, :, :, z_rows, :], "kvz", d, z_dev(d))
    kv[blk, :, :, z_rows, :] = zsend[z, 0:2]
    qd[:, :, z_rows, :] = zsend[z, 2:4]

    pick = lax.broadcasted_iota(jnp.int32, (64, 4), 0) // 16 == lax.broadcasted_iota(
        jnp.int32, (64, 4), 1)
    w_rows[...] = nn(pick.astype(bf16), w_bias[...]).astype(bf16)
    row_in = lax.rem(lax.broadcasted_iota(jnp.int32, (64, 128), 0), 16)

    def tile_step(i, acc):
        for u in range(4):
            jj = i * 4 + u
            tokens = jnp.concatenate([pair[q * 16 + jj] for q in range(4)], axis=0).astype(f32)
            hat, rstd, _ = norm(tokens)
            xhat[jj] = hat
            rstd_all[jj] = jnp.broadcast_to(rstd, (128, 128))
            normed = (hat * gain_v).astype(bf16)
            chosen = jnp.where(row_in == jj, w_rows[...].astype(f32), 0.0).astype(bf16)
            acc = acc + nt(chosen, normed)
        return acc

    tile_bias = lax.fori_loop(0, 4, tile_step, jnp.zeros((64, 128), f32))
    bsend[...] = tile_bias.astype(bf16).reshape(4, 16, 128)
    odd = lax.rem(y, 2)
    turn_own(bsend.at[z], brecv.at[odd, zhi, z], "bt", odd * 8, by_column(0, 0, core))
    for n, c in enumerate((core, other)):
        for e, d in AROUND:
            if (n, e, d) != (0, 0, 0):
                send(bsend.at[z_at(d)], brecv.at[odd, zhi, z], "bt", n * 8 + e * 4 + d,
                     by_column(e, d, c), odd * 8 + e * 4 + d)
    for d in (1, 3, 2):
        send(zsend.at[z_at(d), 2:4], qd.at[:, :, z_rows, :], "qdz", d, z_dev(d))

    for d in (1, 2, 3):
        rows_d = pl.ds(pl.multiple_of(z_at(4 - d) * 32, 32), 32)
        arrived(kv.at[blk, :, :, rows_d, :], "kvz", d)
    for d in (1, 3, 2):
        send(kv.at[blk], kv.at[blk], "kvx", d, x_dev(d))
    send(kv.at[blk], kv.at[blk], "kvc", 0, core_dev)

    for n in range(2):
        for e, d in AROUND:
            arrived(brecv.at[n, lax.rem(zhi + e, 2), z_at(4 - d)], "bt", n * 8 + e * 4 + d)
    for n in range(2):
        for e in range(2):
            outs = lane_swap([brecv[n, e, b].astype(f32) for b in range(4)])
            bias[y, n, e, 0:16] = jnp.where(core == 0, outs[0], outs[2]).astype(bf16)
            bias[y, n, e, 16:32] = jnp.where(core == 0, outs[1], outs[3]).astype(bf16)
    for d in (4, 3, 5, 2, 6, 1, 7):
        send(bias.at[y], bias.at[y], "ya", d, y_dev(d))

    for d in (1, 2, 3):
        rows_d = pl.ds(pl.multiple_of(z_at(4 - d) * 32, 32), 32)
        arrived(qd.at[:, :, rows_d, :], "qdz", d)
    for n in range(2):
        for g in range(2):
            qdt[n, g] = qd[n, g].astype(f32).T.astype(bf16)

    for d in (1, 3, 2):
        k_d = x_at(4 - d) * 2 + core
        arrived(kv.at[k_d], "kvx", d)
        send(kv.at[k_d], kv.at[k_d], "kvc", d, core_dev)
    for d in (0, 1, 3, 2):
        arrived(kv.at[x_at(4 - d) * 2 + other], "kvc", d)

    for d in range(1, 8):
        arrived(bias.at[y_at(8 - d)], "ya", d)

    spot = lax.broadcasted_iota(jnp.int32, (1, 1024), 1)
    spot_c = (lax.div(spot, 256) * 8 + lax.rem(lax.div(spot, 32), 4) * 2
              + lax.rem(lax.div(spot, 128), 2))
    keep = spot_c * 32 + lax.rem(spot, 32) < length[0]
    for b in range(8):
        bias_f[:, b * 128:(b + 1) * 128] = bias[b].reshape(128, 128).astype(f32)
    dbias[...] = jnp.zeros_like(dbias)
    att[...] = jnp.zeros_like(att)
    dqkv[0] = jnp.zeros_like(dqkv[0])
    lanes = lane_block((128, 128))

    def cores_summed(g):
        arrived(dkv_c.at[g], "dkvc", g)
        for b in range(4):
            dkv_m[g, b] = (dkv_send[core, g, b].astype(f32) + dkv_c[g, b].astype(f32)).astype(bf16)
        for d in (1, 3, 2):
            send(dkv_m.at[g, x_at(d)], dkv_in.at[g, d], "dr", g * 4 + d, x_dev(d))

    for g in range(2):
        def attend(a):
            own = lanes == a
            key = kv[:, 0, g].reshape(1024, 128)
            value = kv[:, 1, g].reshape(1024, 128)
            q_a = jnp.where(own, qd[0, g].astype(f32), 0.0).astype(bf16)
            do_f = jnp.where(own, qd[1, g].astype(f32), 0.0)
            do_a = do_f.astype(bf16)
            logits = jnp.where(keep, nt(q_a, key) + bias_f[...], NEG)
            top = jnp.max(logits, axis=-1, keepdims=True)
            expo = jnp.exp(logits - top)
            inv = 1.0 / jnp.sum(expo, axis=-1, keepdims=True)
            out = nn(expo.astype(bf16), value) * inv
            out = jnp.where(own, out, 0.0)
            att[g] = att[g] + out
            delta = jnp.sum(do_f * out, axis=-1, keepdims=True)
            shares = expo * inv
            grads = shares * (nt(do_a, value) - delta)
            for b in range(8):
                dbias[b] = dbias[b] + grads[:, b * 128:(b + 1) * 128]
            grads_b = grads.astype(bf16)
            dq = nn(grads_b, key) * (32 ** (-0.5))
            dqkv[0, g] = jnp.where(own, dq, dqkv[0, g].astype(f32)).astype(bf16)
            part = slice(a * 32, (a + 1) * 32)
            dk = nn(qdt[0, g, part, :], grads_b).astype(bf16)
            dv = nn(qdt[1, g, part, :], shares.astype(bf16)).astype(bf16)
            for b in range(8):
                dkv_send[b % 2, g, b // 2, 0, part, :] = dk[:, b * 128:(b + 1) * 128]
                dkv_send[b % 2, g, b // 2, 1, part, :] = dv[:, b * 128:(b + 1) * 128]

        for a in range(4):
            if (g, a) == (1, 2):
                cores_summed(0)
            attend(a)
        send(dkv_send.at[other, g], dkv_c.at[g], "dkvc", g, core_dev)

    for b in range(8):
        db_send[b] = dbias[b].astype(bf16)
    for d in (4, 3, 5, 2, 6, 1, 7):
        send(db_send.at[y_at(d)], db_y.at[d], "yr", d, y_dev(d))
    for d in (1, 3, 2):
        rows_d = pl.ds(pl.multiple_of(z_at(d) * 32, 32), 32)
        send(att.at[:, rows_d, :], o_in.at[z], "oz", d, z_dev(d))
        send(dqkv.at[0, :, rows_d, :], e_in.at[z, 0], "dqz", d, z_dev(d))
    o_in[z] = att[:, z_rows, :]
    e_in[z, 0] = dqkv[0, :, z_rows, :]

    cores_summed(1)

    total = dbias[y]
    for d in range(1, 8):
        arrived(db_y.at[d], "yr", d)
        total = total + db_y[d].astype(f32)
    db_s[...] = total.reshape(2, 64, 128)
    turn_own(db_s.at[core], db_t.at[core], "dt", core, by_row(core))
    send(db_s.at[other], db_t.at[core], "dt", 1, by_row(other), core)

    for g in range(2):
        for d in (1, 3, 2):
            arrived(dkv_in.at[g, d], "dr", g * 4 + d)
        for n in range(2):
            total = dkv_m[g, x, n].astype(f32)
            for d in (1, 2, 3):
                total = total + dkv_in[g, d, n].astype(f32)
            dqkv[1 + n, g] = total.T.astype(bf16)
    for d in (1, 3, 2):
        rows_d = pl.ds(pl.multiple_of(z_at(d) * 32, 32), 32)
        send(dqkv.at[1:3, :, rows_d, :], e_in.at[z, 1:3], "dkvz", d, z_dev(d))
    e_in[z, 1:3] = dqkv[1:3, :, z_rows, :]

    arrived(db_t.at[0], "dt", 0)
    arrived(db_t.at[1], "dt", 1)
    for e in range(2):
        final = db_t[:, e * 32:(e + 1) * 32, :].reshape(64, 128)
        outs = lane_swap([final[q * 16:(q + 1) * 16] for q in range(4)])
        for b in range(4):
            db_out[e, b] = outs[b]
    for e, d in AROUND[1:]:
        send(db_out.at[lax.rem(zhi + e, 2), z_at(d)], db_in.at[zhi, z], "dbz", e * 4 + d,
             zz_dev(e, d))
    db_in[zhi, z] = db_out[zhi, z]

    for d in (1, 2, 3):
        h_d = z_at(4 - d)
        arrived(o_in.at[h_d], "oz", d)
        arrived(e_in.at[h_d, 0], "dqz", d)
    gated = []
    pres = []
    for g in range(2):
        outs = lane_swap([o_in[h, g] for h in range(4)])
        for i in range(4):
            at = slice((g * 4 + i) * 32, (g * 4 + i + 1) * 32)
            gate_t, gg_t = gate_s[at], gg_s[at]
            gated.append((gate_t * outs[i]).astype(bf16))
            pres.append((gg_t * outs[i] * gate_t * (1.0 - gate_t)).astype(bf16))
    update[...] = nn(jnp.concatenate(gated, axis=0), w_out[...]).astype(bf16).reshape(8, 32, 128)
    for d in (1, 2, 3):
        arrived(e_in.at[z_at(4 - d), 1:3], "dkvz", d)
    sides = [jnp.concatenate(pres, axis=0)]
    for n in range(3):
        tiles = []
        for g in range(2):
            tiles += lane_swap([e_in[h, n, g].astype(f32) for h in range(4)])
        sides.append(jnp.concatenate(tiles, axis=0).astype(bf16))
    grad_window = (nt(sides[1], w_query[...]) + nt(sides[2], w_key[...])
                   + nt(sides[3], w_value[...]) + nt(sides[0], w_gate[...]))
    gw[0:8] = grad_window.reshape(8, 32, 128)
    gw[8:16] = jnp.zeros((8, 32, 128), f32)

    for e, d in AROUND[1:]:
        arrived(db_in.at[lax.rem(zhi + e, 2), z_at(4 - d)], "dbz", e * 4 + d)
    flat = (db_in[0] + db_in[1]).reshape(64, 128).T
    high = flat.astype(bf16)
    rest = flat - high.astype(f32)
    mid = rest.astype(bf16)
    low = (rest - mid.astype(f32)).astype(bf16)

    def final_step(i, carry):
        for u in range(2):
            jj = i * 2 + u
            chosen = jnp.where(row_in == jj, w_rows[...].astype(f32), 0.0).astype(bf16)
            grad = nn(high, chosen) + (nn(mid, chosen) + nn(low, chosen))
            grad = jnp.concatenate([grad[0:32] + gw[jj], grad[32:]], axis=0) * gain_v
            hat = xhat[jj]
            first = jnp.mean(grad, axis=-1, keepdims=True)
            second = jnp.mean(grad * hat, axis=-1, keepdims=True)
            result = rstd_all[jj] * (grad - first - hat * second)
            for q in range(4):
                pair_grad[q * 16 + jj] = result[q * 32:(q + 1) * 32]
        return carry

    lax.fori_loop(0, 8, final_step, 0)

    for copy in sent:
        copy.wait_send()

    @pl.when(jnp.logical_not(stays))
    def _():
        for copy in turned:
            copy.wait_send()


def body(pair, length, ln_gain, w_query, w_key, w_value, w_gate, w_bias, w_out, out_grad):
    vmem = pl.BlockSpec(memory_space=pltpu.VMEM)
    hbm = pl.BlockSpec(memory_space=pltpu.HBM)
    smem = pl.BlockSpec(memory_space=pltpu.SMEM)

    scratch = [
        pltpu.VMEM(pair.shape, bf16),
        *[pltpu.VMEM((128, 128), bf16) for _ in range(5)],
        pltpu.VMEM(out_grad.shape, bf16),
        pltpu.SemaphoreType.DMA((7,)),
        pltpu.VMEM((16, 128, 128), f32),
        pltpu.VMEM((16, 128, 128), f32),
        pltpu.VMEM((64, 128), bf16),
        pltpu.VMEM((256, 128), f32),
        pltpu.VMEM((256, 128), f32),
        pltpu.VMEM((4, 4, 2, 32, 128), bf16),
        pltpu.VMEM((8, 2, 2, 128, 128), bf16),
        pltpu.VMEM((2, 2, 128, 128), bf16),
        pltpu.VMEM((2, 2, 128, 128), bf16),
        pltpu.VMEM((4, 16, 128), bf16),
        pltpu.VMEM((2, 2, 4, 16, 128), bf16),
        pltpu.VMEM((8, 2, 2, 32, 128), bf16),
        pltpu.VMEM((128, 1024), f32),
        pltpu.VMEM((8, 128, 128), f32),
        pltpu.VMEM((2, 128, 128), f32),
        pltpu.VMEM((3, 2, 128, 128), bf16),
        pltpu.VMEM((8, 128, 128), bf16),
        pltpu.VMEM((8, 128, 128), bf16),
        pltpu.VMEM((2, 64, 128), f32),
        pltpu.VMEM((2, 64, 128), f32),
        pltpu.VMEM((2, 4, 16, 128), f32),
        pltpu.VMEM((2, 4, 16, 128), f32),
        pltpu.VMEM((2, 2, 4, 2, 128, 128), bf16),
        pltpu.VMEM((2, 4, 2, 128, 128), bf16),
        pltpu.VMEM((2, 4, 2, 128, 128), bf16),
        pltpu.VMEM((2, 4, 2, 128, 128), bf16),
        pltpu.VMEM((4, 3, 2, 32, 128), bf16),
        pltpu.VMEM((4, 2, 32, 128), f32),
        pltpu.VMEM((16, 32, 128), f32),
    ]
    for _, n in COPIES:
        scratch += [pltpu.SemaphoreType.DMA((n,)), pltpu.SemaphoreType.DMA((n,))]
    call = pl.pallas_call(
        kernel,
        out_shape=(
            jax.ShapeDtypeStruct(out_grad.shape, bf16),
            jax.ShapeDtypeStruct(pair.shape, f32),
        ),
        in_specs=[hbm, smem, vmem, hbm, hbm, hbm, hbm, vmem, hbm, hbm],
        out_specs=(vmem, vmem),
        scratch_shapes=scratch,
        compiler_params=pltpu.CompilerParams(
            collective_id=0, has_side_effects=True, vmem_limit_bytes=63 * 1024 * 1024
        ),
    )
    return call(
        pair, length, ln_gain.reshape(1, 128), w_query, w_key, w_value, w_gate, w_bias.T, w_out,
        out_grad,
    )


def solution(mesh):
    tiled = P("rows", "cols", None)
    placed = (tiled, P(), P(), P(), P(), P(), P(), P(), P(), tiled)
    return jax.shard_map(
        body, mesh=mesh, in_specs=placed, out_specs=(tiled, tiled), check_vma=False
    )
```

```python
import jax
import jax.numpy as jnp
from jax import lax
from jax.experimental import pallas as pl
from jax.experimental.pallas import tpu as pltpu
from jax.sharding import PartitionSpec as P

EPS = 1e-05
NEG = -1000000000.0
MESH = pl.DeviceIdType.MESH
f32 = jnp.float32
bf16 = jnp.bfloat16
COPIES = (
    ("kvz", 4), ("qdz", 4), ("bt", 16), ("kvx", 4), ("kvc", 4), ("ya", 8), ("dkvc", 2), ("dr", 8),
    ("yr", 8), ("dt", 2), ("dbz", 8), ("oz", 4), ("dqz", 4), ("dkvz", 4),
)

AROUND = ((0, 0), (0, 1), (0, 3), (0, 2), (1, 0), (1, 1), (1, 3), (1, 2))


def nn(left, right):
    return lax.dot_general(left, right, (((1,), (0,)), ((), ())), preferred_element_type=f32)


def nt(left, right):
    return lax.dot_general(left, right, (((1,), (1,)), ((), ())), preferred_element_type=f32)


def lane_block(shape):
    return lax.shift_right_logical(lax.broadcasted_iota(jnp.int32, shape, len(shape) - 1), 5)


def lane_swap(tiles):
    block = lane_block(tiles[0].shape)
    outs = []
    for i in range(4):
        acc = None
        for b in range(4):
            shift = (32 * (b - i)) % 128
            moved = tiles[b] if shift == 0 else pltpu.roll(tiles[b], shift, 1)
            acc = moved if acc is None else jnp.where(block == b, moved, acc)
        outs.append(acc)
    return outs


def remote(src, dst, send_sem, recv_sem, device):
    return pltpu.make_async_remote_copy(
        src_ref=src, dst_ref=dst, send_sem=send_sem, recv_sem=recv_sem,
        device_id=device, device_id_type=MESH,
    )


def kernel(
    pair_h, length, gain, w_query_h, w_key_h, w_value_h, w_gate_h, w_bias, w_out_h, out_grad_h,
    update, pair_grad,
    pair, w_query, w_key, w_value, w_gate, w_out, out_grad, load_sem, xhat, rstd_all, w_rows, gate_s, gg_s, zsend, kv, qd, qdt, bsend, brecv, bias, bias_f,
    dbias, att, dqkv, db_send, db_y, db_s, db_t, db_out, db_in, dkv_send, dkv_c, dkv_m, dkv_in,
    e_in, o_in, gw,
    *sems,
):
    sem = {name: sems[2 * n:2 * n + 2] for n, (name, _) in enumerate(COPIES)}
    row = lax.axis_index("rows")
    col = lax.axis_index("cols")
    y, zhi = lax.div(row, 2), lax.rem(row, 2)
    x, z, core = lax.div(col, 8), lax.rem(lax.div(col, 2), 4), lax.rem(col, 2)
    blk = x * 2 + core
    other = 1 - core

    def device(row_, x_, z_, core_):
        return {"rows": row_, "cols": x_ * 8 + z_ * 2 + core_}

    def z_at(d):
        return lax.rem(z + d, 4)

    def z_dev(d):
        return device(row, x, z_at(d), core)

    def x_at(d):
        return lax.rem(x + d, 4)

    def x_dev(d):
        return device(row, x_at(d), z, core)

    def y_at(d):
        return lax.rem(y + d, 8)

    def y_dev(d):
        return device(y_at(d) * 2 + zhi, x, z, core)

    def zz_dev(e, d):
        return device(y * 2 + lax.rem(zhi + e, 2), x, z_at(d), core)

    def by_column(e, d, c):
        return device(blk * 2 + lax.rem(zhi + e, 2), lax.div(y, 2), z_at(d), c)

    def by_row_all(e, d, s):
        return device(
            (x * 2 + s) * 2 + lax.rem(zhi + e, 2), lax.div(y, 2), z_at(d), lax.rem(y, 2))

    def by_row(s):
        return device((x * 2 + s) * 2 + zhi, lax.div(y, 2), z, lax.rem(y, 2))

    core_dev = device(row, x, z, other)
    stays = blk == y

    sent = []
    turned = []

    def send(src, dst, name, n, dev, at=None):
        copy = remote(src, dst, sem[name][0].at[n], sem[name][1].at[n if at is None else at], dev)
        copy.start()
        sent.append(copy)

    def turn_own(src, dst, name, at, dev):
        away = remote(src, dst, sem[name][0].at[0], sem[name][1].at[at], dev)
        here = pltpu.make_async_copy(src, dst, sem[name][1].at[at])

        @pl.when(stays)
        def _():
            here.start()

        @pl.when(jnp.logical_not(stays))
        def _():
            away.start()

        turned.append(away)

    def arrived(slot, name, n):
        remote(slot, slot, sem[name][0].at[n], sem[name][1].at[n], core_dev).wait_recv()

    barrier = pltpu.get_barrier_semaphore()
    turns = [(e, d, other) for e in range(2) for d in range(4)]
    turns += [(e, d, core) for e in range(2) for d in range(4) if (e, d) != (0, 0)]
    partners = [by_row_all(*turn) for turn in reversed(turns)] + [by_column(0, 0, other)]
    partners += [y_dev(d) for d in (4, 3, 5, 2, 6, 1, 7)] + [x_dev(d) for d in (2, 1, 3)]
    partners += [zz_dev(e, d) for e, d in reversed(AROUND[1:])] + [core_dev]

    def greet(dev):
        pl.semaphore_signal(barrier, inc=1, device_id=dev, device_id_type=MESH)

    @pl.when(jnp.logical_not(stays))
    def _():
        greet(by_column(0, 0, core))
        greet(by_row(core))

    for dev in partners:
        greet(dev)

    loads = [
        pltpu.make_async_copy(src, dst, load_sem.at[n])
        for n, (src, dst) in enumerate((
            (pair_h, pair), (w_query_h, w_query), (w_key_h, w_key), (w_value_h, w_value),
            (w_gate_h, w_gate), (w_out_h, w_out), (out_grad_h, out_grad)))
    ]
    for copy in loads:
        copy.start()

    gain_v = gain[...]
    for copy in loads:
        copy.wait()

    def norm(values):
        average = jnp.mean(values, axis=-1, keepdims=True)
        centred = values - average
        variance = jnp.mean(centred * centred, axis=-1, keepdims=True)
        rstd = lax.rsqrt(variance + EPS)
        return centred * rstd, rstd, centred

    win = pair[0:8].reshape(256, 128).astype(f32)
    hat, _, _ = norm(win)
    window = (hat * gain_v).astype(bf16)
    query = (nn(window, w_query[...]) * (32 ** (-0.5))).astype(bf16).astype(f32)
    keys = nn(window, w_key[...]).astype(bf16).astype(f32)
    vals = nn(window, w_value[...]).astype(bf16).astype(f32)
    gate = jax.nn.sigmoid(nn(window, w_gate[...])).astype(bf16).astype(f32)
    gg = nt(out_grad[...].reshape(256, 128), w_out[...])
    ga = (gg * gate).astype(bf16).astype(f32)
    gate_s[...] = gate
    gg_s[...] = gg
    for n, array in enumerate((keys, vals, query, ga)):
        for g in range(2):
            outs = lane_swap([array[(g * 4 + b) * 32:(g * 4 + b + 1) * 32] for b in range(4)])
            for h in range(4):
                zsend[h, n, g] = outs[h].astype(bf16)

    pick = lax.broadcasted_iota(jnp.int32, (64, 4), 0) // 16 == lax.broadcasted_iota(
        jnp.int32, (64, 4), 1)
    w_rows[...] = nn(pick.astype(bf16), w_bias[...]).astype(bf16)
    row_in = lax.rem(lax.broadcasted_iota(jnp.int32, (64, 128), 0), 16)

    def tile_step(i, acc):
        for u in range(4):
            jj = i * 4 + u
            tokens = jnp.concatenate([pair[q * 16 + jj] for q in range(4)], axis=0).astype(f32)
            hat, rstd, _ = norm(tokens)
            xhat[jj] = hat
            rstd_all[jj] = jnp.broadcast_to(rstd, (128, 128))
            normed = (hat * gain_v).astype(bf16)
            chosen = jnp.where(row_in == jj, w_rows[...].astype(f32), 0.0).astype(bf16)
            acc = acc + nt(chosen, normed)
        return acc

    tile_bias = lax.fori_loop(0, 4, tile_step, jnp.zeros((64, 128), f32))
    bsend[...] = tile_bias.astype(bf16).reshape(4, 16, 128)
    pl.semaphore_wait(barrier, len(partners) + jnp.where(stays, 0, 2))

    z_rows = pl.ds(pl.multiple_of(z * 32, 32), 32)
    for d in (1, 3, 2):
        send(zsend.at[z_at(d), 0:2], kv.at[blk, :, :, z_rows, :], "kvz", d, z_dev(d))
    kv[blk, :, :, z_rows, :] = zsend[z, 0:2]
    qd[:, :, z_rows, :] = zsend[z, 2:4]

    odd = lax.rem(y, 2)
    turn_own(bsend.at[z], brecv.at[odd, zhi, z], "bt", odd * 8, by_column(0, 0, core))
    for n, c in enumerate((core, other)):
        for e, d in AROUND:
            if (n, e, d) != (0, 0, 0):
                send(bsend.at[z_at(d)], brecv.at[odd, zhi, z], "bt", n * 8 + e * 4 + d,
                     by_column(e, d, c), odd * 8 + e * 4 + d)
    for d in (1, 3, 2):
        send(zsend.at[z_at(d), 2:4], qd.at[:, :, z_rows, :], "qdz", d, z_dev(d))

    for d in (1, 2, 3):
        rows_d = pl.ds(pl.multiple_of(z_at(4 - d) * 32, 32), 32)
        arrived(kv.at[blk, :, :, rows_d, :], "kvz", d)
    for d in (1, 3, 2):
        send(kv.at[blk], kv.at[blk], "kvx", d, x_dev(d))
    send(kv.at[blk], kv.at[blk], "kvc", 0, core_dev)

    for n in range(2):
        for e, d in AROUND:
            arrived(brecv.at[n, lax.rem(zhi + e, 2), z_at(4 - d)], "bt", n * 8 + e * 4 + d)
    for n in range(2):
        for e in range(2):
            outs = lane_swap([brecv[n, e, b].astype(f32) for b in range(4)])
            bias[y, n, e, 0:16] = jnp.where(core == 0, outs[0], outs[2]).astype(bf16)
            bias[y, n, e, 16:32] = jnp.where(core == 0, outs[1], outs[3]).astype(bf16)
    for d in (4, 3, 5, 2, 6, 1, 7):
        send(bias.at[y], bias.at[y], "ya", d, y_dev(d))

    for d in (1, 2, 3):
        rows_d = pl.ds(pl.multiple_of(z_at(4 - d) * 32, 32), 32)
        arrived(qd.at[:, :, rows_d, :], "qdz", d)
    for n in range(2):
        for g in range(2):
            qdt[n, g] = qd[n, g].astype(f32).T.astype(bf16)

    for d in (1, 3, 2):
        k_d = x_at(4 - d) * 2 + core
        arrived(kv.at[k_d], "kvx", d)
        send(kv.at[k_d], kv.at[k_d], "kvc", d, core_dev)
    for d in (0, 1, 3, 2):
        arrived(kv.at[x_at(4 - d) * 2 + other], "kvc", d)

    for d in range(1, 8):
        arrived(bias.at[y_at(8 - d)], "ya", d)

    spot = lax.broadcasted_iota(jnp.int32, (1, 1024), 1)
    spot_c = (lax.div(spot, 256) * 8 + lax.rem(lax.div(spot, 32), 4) * 2
              + lax.rem(lax.div(spot, 128), 2))
    keep = spot_c * 32 + lax.rem(spot, 32) < length[0]
    for b in range(8):
        bias_f[:, b * 128:(b + 1) * 128] = bias[b].reshape(128, 128).astype(f32)
    dbias[...] = jnp.zeros_like(dbias)
    att[...] = jnp.zeros_like(att)
    dqkv[0] = jnp.zeros_like(dqkv[0])
    lanes = lane_block((128, 128))

    def cores_summed(g):
        arrived(dkv_c.at[g], "dkvc", g)
        for b in range(4):
            dkv_m[g, b] = (dkv_send[core, g, b].astype(f32) + dkv_c[g, b].astype(f32)).astype(bf16)
        for d in (1, 3, 2):
            send(dkv_m.at[g, x_at(d)], dkv_in.at[g, d], "dr", g * 4 + d, x_dev(d))

    for g in range(2):
        def attend(a):
            own = lanes == a
            key = kv[:, 0, g].reshape(1024, 128)
            value = kv[:, 1, g].reshape(1024, 128)
            q_a = jnp.where(own, qd[0, g].astype(f32), 0.0).astype(bf16)
            do_f = jnp.where(own, qd[1, g].astype(f32), 0.0)
            do_a = do_f.astype(bf16)
            logits = jnp.where(keep, nt(q_a, key) + bias_f[...], NEG)
            top = jnp.max(logits, axis=-1, keepdims=True)
            expo = jnp.exp(logits - top)
            inv = 1.0 / jnp.sum(expo, axis=-1, keepdims=True)
            out = nn(expo.astype(bf16), value) * inv
            out = jnp.where(own, out, 0.0)
            att[g] = att[g] + out
            delta = jnp.sum(do_f * out, axis=-1, keepdims=True)
            shares = expo * inv
            grads = shares * (nt(do_a, value) - delta)
            for b in range(8):
                dbias[b] = dbias[b] + grads[:, b * 128:(b + 1) * 128]
            grads_b = grads.astype(bf16)
            dq = nn(grads_b, key) * (32 ** (-0.5))
            dqkv[0, g] = jnp.where(own, dq, dqkv[0, g].astype(f32)).astype(bf16)
            part = slice(a * 32, (a + 1) * 32)
            dk = nn(qdt[0, g, part, :], grads_b).astype(bf16)
            dv = nn(qdt[1, g, part, :], shares.astype(bf16)).astype(bf16)
            for b in range(8):
                dkv_send[b % 2, g, b // 2, 0, part, :] = dk[:, b * 128:(b + 1) * 128]
                dkv_send[b % 2, g, b // 2, 1, part, :] = dv[:, b * 128:(b + 1) * 128]

        for a in range(4):
            if (g, a) == (1, 2):
                cores_summed(0)
            attend(a)
        send(dkv_send.at[other, g], dkv_c.at[g], "dkvc", g, core_dev)

    for b in range(8):
        db_send[b] = dbias[b].astype(bf16)
    for d in (4, 3, 5, 2, 6, 1, 7):
        send(db_send.at[y_at(d)], db_y.at[d], "yr", d, y_dev(d))
    for d in (1, 3, 2):
        rows_d = pl.ds(pl.multiple_of(z_at(d) * 32, 32), 32)
        send(att.at[:, rows_d, :], o_in.at[z], "oz", d, z_dev(d))
        send(dqkv.at[0, :, rows_d, :], e_in.at[z, 0], "dqz", d, z_dev(d))
    o_in[z] = att[:, z_rows, :]
    e_in[z, 0] = dqkv[0, :, z_rows, :]

    cores_summed(1)

    total = dbias[y]
    for d in range(1, 8):
        arrived(db_y.at[d], "yr", d)
        total = total + db_y[d].astype(f32)
    db_s[...] = total.reshape(2, 64, 128)
    turn_own(db_s.at[core], db_t.at[core], "dt", core, by_row(core))
    send(db_s.at[other], db_t.at[core], "dt", 1, by_row(other), core)

    for g in range(2):
        for d in (1, 3, 2):
            arrived(dkv_in.at[g, d], "dr", g * 4 + d)
        for n in range(2):
            total = dkv_m[g, x, n].astype(f32)
            for d in (1, 2, 3):
                total = total + dkv_in[g, d, n].astype(f32)
            dqkv[1 + n, g] = total.T.astype(bf16)
    for d in (1, 3, 2):
        rows_d = pl.ds(pl.multiple_of(z_at(d) * 32, 32), 32)
        send(dqkv.at[1:3, :, rows_d, :], e_in.at[z, 1:3], "dkvz", d, z_dev(d))
    e_in[z, 1:3] = dqkv[1:3, :, z_rows, :]

    arrived(db_t.at[0], "dt", 0)
    arrived(db_t.at[1], "dt", 1)
    for e in range(2):
        final = db_t[:, e * 32:(e + 1) * 32, :].reshape(64, 128)
        outs = lane_swap([final[q * 16:(q + 1) * 16] for q in range(4)])
        for b in range(4):
            db_out[e, b] = outs[b]
    for e, d in AROUND[1:]:
        send(db_out.at[lax.rem(zhi + e, 2), z_at(d)], db_in.at[zhi, z], "dbz", e * 4 + d,
             zz_dev(e, d))
    db_in[zhi, z] = db_out[zhi, z]

    for d in (1, 2, 3):
        h_d = z_at(4 - d)
        arrived(o_in.at[h_d], "oz", d)
        arrived(e_in.at[h_d, 0], "dqz", d)
    gated = []
    pres = []
    for g in range(2):
        outs = lane_swap([o_in[h, g] for h in range(4)])
        for i in range(4):
            at = slice((g * 4 + i) * 32, (g * 4 + i + 1) * 32)
            gate_t, gg_t = gate_s[at], gg_s[at]
            gated.append((gate_t * outs[i]).astype(bf16))
            pres.append((gg_t * outs[i] * gate_t * (1.0 - gate_t)).astype(bf16))
    update[...] = nn(jnp.concatenate(gated, axis=0), w_out[...]).astype(bf16).reshape(8, 32, 128)
    for d in (1, 2, 3):
        arrived(e_in.at[z_at(4 - d), 1:3], "dkvz", d)
    sides = [jnp.concatenate(pres, axis=0)]
    for n in range(3):
        tiles = []
        for g in range(2):
            tiles += lane_swap([e_in[h, n, g].astype(f32) for h in range(4)])
        sides.append(jnp.concatenate(tiles, axis=0).astype(bf16))
    grad_window = (nt(sides[1], w_query[...]) + nt(sides[2], w_key[...])
                   + nt(sides[3], w_value[...]) + nt(sides[0], w_gate[...]))
    gw[0:8] = grad_window.reshape(8, 32, 128)
    gw[8:16] = jnp.zeros((8, 32, 128), f32)

    for e, d in AROUND[1:]:
        arrived(db_in.at[lax.rem(zhi + e, 2), z_at(4 - d)], "dbz", e * 4 + d)
    flat = (db_in[0] + db_in[1]).reshape(64, 128).T
    high = flat.astype(bf16)
    rest = flat - high.astype(f32)
    mid = rest.astype(bf16)
    low = (rest - mid.astype(f32)).astype(bf16)

    def final_step(i, carry):
        for u in range(2):
            jj = i * 2 + u
            chosen = jnp.where(row_in == jj, w_rows[...].astype(f32), 0.0).astype(bf16)
            grad = nn(high, chosen) + (nn(mid, chosen) + nn(low, chosen))
            grad = jnp.concatenate([grad[0:32] + gw[jj], grad[32:]], axis=0) * gain_v
            hat = xhat[jj]
            first = jnp.mean(grad, axis=-1, keepdims=True)
            second = jnp.mean(grad * hat, axis=-1, keepdims=True)
            result = rstd_all[jj] * (grad - first - hat * second)
            for q in range(4):
                pair_grad[q * 16 + jj] = result[q * 32:(q + 1) * 32]
        return carry

    lax.fori_loop(0, 8, final_step, 0)

    for copy in sent:
        copy.wait_send()

    @pl.when(jnp.logical_not(stays))
    def _():
        for copy in turned:
            copy.wait_send()


def body(pair, length, ln_gain, w_query, w_key, w_value, w_gate, w_bias, w_out, out_grad):
    vmem = pl.BlockSpec(memory_space=pltpu.VMEM)
    hbm = pl.BlockSpec(memory_space=pltpu.HBM)
    smem = pl.BlockSpec(memory_space=pltpu.SMEM)

    scratch = [
        pltpu.VMEM(pair.shape, bf16),
        *[pltpu.VMEM((128, 128), bf16) for _ in range(5)],
        pltpu.VMEM(out_grad.shape, bf16),
        pltpu.SemaphoreType.DMA((7,)),
        pltpu.VMEM((16, 128, 128), f32),
        pltpu.VMEM((16, 128, 128), f32),
        pltpu.VMEM((64, 128), bf16),
        pltpu.VMEM((256, 128), f32),
        pltpu.VMEM((256, 128), f32),
        pltpu.VMEM((4, 4, 2, 32, 128), bf16),
        pltpu.VMEM((8, 2, 2, 128, 128), bf16),
        pltpu.VMEM((2, 2, 128, 128), bf16),
        pltpu.VMEM((2, 2, 128, 128), bf16),
        pltpu.VMEM((4, 16, 128), bf16),
        pltpu.VMEM((2, 2, 4, 16, 128), bf16),
        pltpu.VMEM((8, 2, 2, 32, 128), bf16),
        pltpu.VMEM((128, 1024), f32),
        pltpu.VMEM((8, 128, 128), f32),
        pltpu.VMEM((2, 128, 128), f32),
        pltpu.VMEM((3, 2, 128, 128), bf16),
        pltpu.VMEM((8, 128, 128), bf16),
        pltpu.VMEM((8, 128, 128), bf16),
        pltpu.VMEM((2, 64, 128), f32),
        pltpu.VMEM((2, 64, 128), f32),
        pltpu.VMEM((2, 4, 16, 128), f32),
        pltpu.VMEM((2, 4, 16, 128), f32),
        pltpu.VMEM((2, 2, 4, 2, 128, 128), bf16),
        pltpu.VMEM((2, 4, 2, 128, 128), bf16),
        pltpu.VMEM((2, 4, 2, 128, 128), bf16),
        pltpu.VMEM((2, 4, 2, 128, 128), bf16),
        pltpu.VMEM((4, 3, 2, 32, 128), bf16),
        pltpu.VMEM((4, 2, 32, 128), f32),
        pltpu.VMEM((16, 32, 128), f32),
    ]
    for _, n in COPIES:
        scratch += [pltpu.SemaphoreType.DMA((n,)), pltpu.SemaphoreType.DMA((n,))]
    call = pl.pallas_call(
        kernel,
        out_shape=(
            jax.ShapeDtypeStruct(out_grad.shape, bf16),
            jax.ShapeDtypeStruct(pair.shape, f32),
        ),
        in_specs=[hbm, smem, vmem, hbm, hbm, hbm, hbm, vmem, hbm, hbm],
        out_specs=(vmem, vmem),
        scratch_shapes=scratch,
        compiler_params=pltpu.CompilerParams(
            collective_id=0, has_side_effects=True, vmem_limit_bytes=63 * 1024 * 1024
        ),
    )
    return call(
        pair, length, ln_gain.reshape(1, 128), w_query, w_key, w_value, w_gate, w_bias.T, w_out,
        out_grad,
    )


def solution(mesh):
    tiled = P("rows", "cols", None)
    placed = (tiled, P(), P(), P(), P(), P(), P(), P(), P(), tiled)
    return jax.shard_map(
        body, mesh=mesh, in_specs=placed, out_specs=(tiled, tiled), check_vma=False
    )
```

```python
import jax
import jax.numpy as jnp
from jax import lax
from jax.experimental import pallas as pl
from jax.experimental.pallas import tpu as pltpu
from jax.sharding import PartitionSpec as P

EPS = 1e-05
NEG = -1000000000.0
MESH = pl.DeviceIdType.MESH
f32 = jnp.float32
bf16 = jnp.bfloat16
COPIES = (
    ("kvz", 4), ("qdz", 4), ("bt", 16), ("kvx", 4), ("kvc", 4), ("ya", 8), ("dkvc", 2), ("dr", 8),
    ("yr", 8), ("dt", 2), ("dbz", 8), ("oz", 4), ("dqz", 4), ("dkvz", 4),
)

AROUND = ((0, 0), (0, 1), (0, 3), (0, 2), (1, 0), (1, 1), (1, 3), (1, 2))


def nn(left, right):
    return lax.dot_general(left, right, (((1,), (0,)), ((), ())), preferred_element_type=f32)


def nt(left, right):
    return lax.dot_general(left, right, (((1,), (1,)), ((), ())), preferred_element_type=f32)


def lane_block(shape):
    return lax.shift_right_logical(lax.broadcasted_iota(jnp.int32, shape, len(shape) - 1), 5)


def lane_swap(tiles):
    block = lane_block(tiles[0].shape)
    outs = []
    for i in range(4):
        acc = None
        for b in range(4):
            shift = (32 * (b - i)) % 128
            moved = tiles[b] if shift == 0 else pltpu.roll(tiles[b], shift, 1)
            acc = moved if acc is None else jnp.where(block == b, moved, acc)
        outs.append(acc)
    return outs


def remote(src, dst, send_sem, recv_sem, device):
    return pltpu.make_async_remote_copy(
        src_ref=src, dst_ref=dst, send_sem=send_sem, recv_sem=recv_sem,
        device_id=device, device_id_type=MESH,
    )


def kernel(
    pair_h, length, gain, w_query_h, w_key_h, w_value_h, w_gate_h, w_bias, w_out_h, out_grad_h,
    update, pair_grad,
    pair, w_query, w_key, w_value, w_gate, w_out, out_grad, load_sem, xhat, rstd_all, w_rows, gate_s, gg_s, zsend, kv, qd, qdt, bsend, brecv, bias, bias_f,
    dbias, att, dqkv, db_send, db_y, db_s, db_t, db_out, db_in, dkv_send, dkv_c, dkv_m, dkv_in,
    e_in, o_in, gw, raw_s, raw_p, grads_s, shares_s, result_s, leave_sem,
    *sems,
):
    sem = {name: sems[2 * n:2 * n + 2] for n, (name, _) in enumerate(COPIES)}
    row = lax.axis_index("rows")
    col = lax.axis_index("cols")
    y, zhi = lax.div(row, 2), lax.rem(row, 2)
    x, z, core = lax.div(col, 8), lax.rem(lax.div(col, 2), 4), lax.rem(col, 2)
    blk = x * 2 + core
    other = 1 - core

    def device(row_, x_, z_, core_):
        return {"rows": row_, "cols": x_ * 8 + z_ * 2 + core_}

    def z_at(d):
        return lax.rem(z + d, 4)

    def z_dev(d):
        return device(row, x, z_at(d), core)

    def x_at(d):
        return lax.rem(x + d, 4)

    def x_dev(d):
        return device(row, x_at(d), z, core)

    def y_at(d):
        return lax.rem(y + d, 8)

    def y_dev(d):
        return device(y_at(d) * 2 + zhi, x, z, core)

    def zz_dev(e, d):
        return device(y * 2 + lax.rem(zhi + e, 2), x, z_at(d), core)

    def by_column(e, d, c):
        return device(blk * 2 + lax.rem(zhi + e, 2), lax.div(y, 2), z_at(d), c)

    def by_row_all(e, d, s):
        return device(
            (x * 2 + s) * 2 + lax.rem(zhi + e, 2), lax.div(y, 2), z_at(d), lax.rem(y, 2))

    def by_row(s):
        return device((x * 2 + s) * 2 + zhi, lax.div(y, 2), z, lax.rem(y, 2))

    core_dev = device(row, x, z, other)
    stays = blk == y

    sent = []
    turned = []

    def send(src, dst, name, n, dev, at=None):
        copy = remote(src, dst, sem[name][0].at[n], sem[name][1].at[n if at is None else at], dev)
        copy.start()
        sent.append(copy)

    def turn_own(src, dst, name, at, dev):
        away = remote(src, dst, sem[name][0].at[0], sem[name][1].at[at], dev)
        here = pltpu.make_async_copy(src, dst, sem[name][1].at[at])

        @pl.when(stays)
        def _():
            here.start()

        @pl.when(jnp.logical_not(stays))
        def _():
            away.start()

        turned.append(away)

    def arrived(slot, name, n):
        remote(slot, slot, sem[name][0].at[n], sem[name][1].at[n], core_dev).wait_recv()

    barrier = pltpu.get_barrier_semaphore()
    turns = [(e, d, other) for e in range(2) for d in range(4)]
    turns += [(e, d, core) for e in range(2) for d in range(4) if (e, d) != (0, 0)]
    partners = [by_row_all(*turn) for turn in reversed(turns)] + [by_column(0, 0, other)]
    partners += [y_dev(d) for d in (4, 3, 5, 2, 6, 1, 7)] + [x_dev(d) for d in (2, 1, 3)]
    partners += [zz_dev(e, d) for e, d in reversed(AROUND[1:])] + [core_dev]

    def greet(dev):
        pl.semaphore_signal(barrier, inc=1, device_id=dev, device_id_type=MESH)

    @pl.when(jnp.logical_not(stays))
    def _():
        greet(by_column(0, 0, core))
        greet(by_row(core))

    for dev in partners:
        greet(dev)

    loads = [
        pltpu.make_async_copy(src, dst, load_sem.at[n])
        for n, (src, dst) in enumerate((
            (pair_h, pair), (w_query_h, w_query), (w_key_h, w_key), (w_value_h, w_value),
            (w_gate_h, w_gate), (w_out_h, w_out), (out_grad_h, out_grad)))
    ]
    for copy in loads:
        copy.start()

    gain_v = gain[...]
    for copy in loads:
        copy.wait()

    def norm(values):
        average = jnp.mean(values, axis=-1, keepdims=True)
        centred = values - average
        variance = jnp.mean(centred * centred, axis=-1, keepdims=True)
        rstd = lax.rsqrt(variance + EPS)
        return centred * rstd, rstd, centred

    win = pair[0:8].reshape(256, 128).astype(f32)
    hat, _, _ = norm(win)
    window = (hat * gain_v).astype(bf16)
    query = (nn(window, w_query[...]) * (32 ** (-0.5))).astype(bf16).astype(f32)
    keys = nn(window, w_key[...]).astype(bf16).astype(f32)
    vals = nn(window, w_value[...]).astype(bf16).astype(f32)
    gate = jax.nn.sigmoid(nn(window, w_gate[...])).astype(bf16).astype(f32)
    gg = nt(out_grad[...].reshape(256, 128), w_out[...])
    ga = (gg * gate).astype(bf16).astype(f32)
    gate_s[...] = gate
    gg_s[...] = gg
    for n, array in enumerate((keys, vals, query, ga)):
        for g in range(2):
            outs = lane_swap([array[(g * 4 + b) * 32:(g * 4 + b + 1) * 32] for b in range(4)])
            for h in range(4):
                zsend[h, n, g] = outs[h].astype(bf16)

    pick = lax.broadcasted_iota(jnp.int32, (64, 4), 0) // 16 == lax.broadcasted_iota(
        jnp.int32, (64, 4), 1)
    w_rows[...] = nn(pick.astype(bf16), w_bias[...]).astype(bf16)
    row_in = lax.rem(lax.broadcasted_iota(jnp.int32, (64, 128), 0), 16)

    def tile_step(i, acc):
        for u in range(4):
            jj = i * 4 + u
            tokens = jnp.concatenate([pair[q * 16 + jj] for q in range(4)], axis=0).astype(f32)
            hat, rstd, _ = norm(tokens)
            xhat[jj] = hat
            rstd_all[jj] = jnp.broadcast_to(rstd, (128, 128))
            normed = (hat * gain_v).astype(bf16)
            chosen = jnp.where(row_in == jj, w_rows[...].astype(f32), 0.0).astype(bf16)
            acc = acc + nt(chosen, normed)
        return acc

    tile_bias = lax.fori_loop(0, 4, tile_step, jnp.zeros((64, 128), f32))
    bsend[...] = tile_bias.astype(bf16).reshape(4, 16, 128)
    pl.semaphore_wait(barrier, len(partners) + jnp.where(stays, 0, 2))

    z_rows = pl.ds(pl.multiple_of(z * 32, 32), 32)
    for d in (1, 3, 2):
        send(zsend.at[z_at(d), 0:2], kv.at[blk, :, :, z_rows, :], "kvz", d, z_dev(d))
    kv[blk, :, :, z_rows, :] = zsend[z, 0:2]
    qd[:, :, z_rows, :] = zsend[z, 2:4]

    odd = lax.rem(y, 2)
    turn_own(bsend.at[z], brecv.at[odd, zhi, z], "bt", odd * 8, by_column(0, 0, core))
    for n, c in enumerate((core, other)):
        for e, d in AROUND:
            if (n, e, d) != (0, 0, 0):
                send(bsend.at[z_at(d)], brecv.at[odd, zhi, z], "bt", n * 8 + e * 4 + d,
                     by_column(e, d, c), odd * 8 + e * 4 + d)
    for d in (1, 3, 2):
        send(zsend.at[z_at(d), 2:4], qd.at[:, :, z_rows, :], "qdz", d, z_dev(d))

    for d in (1, 2, 3):
        rows_d = pl.ds(pl.multiple_of(z_at(4 - d) * 32, 32), 32)
        arrived(kv.at[blk, :, :, rows_d, :], "kvz", d)
    for d in (1, 3, 2):
        send(kv.at[blk], kv.at[blk], "kvx", d, x_dev(d))
    send(kv.at[blk], kv.at[blk], "kvc", 0, core_dev)

    for n in range(2):
        for e, d in AROUND:
            arrived(brecv.at[n, lax.rem(zhi + e, 2), z_at(4 - d)], "bt", n * 8 + e * 4 + d)
    for n in range(2):
        for e in range(2):
            outs = lane_swap([brecv[n, e, b].astype(f32) for b in range(4)])
            bias[y, n, e, 0:16] = jnp.where(core == 0, outs[0], outs[2]).astype(bf16)
            bias[y, n, e, 16:32] = jnp.where(core == 0, outs[1], outs[3]).astype(bf16)
    for d in (4, 3, 5, 2, 6, 1, 7):
        send(bias.at[y], bias.at[y], "ya", d, y_dev(d))

    for d in (1, 2, 3):
        rows_d = pl.ds(pl.multiple_of(z_at(4 - d) * 32, 32), 32)
        arrived(qd.at[:, :, rows_d, :], "qdz", d)
    for n in range(2):
        for g in range(2):
            qdt[n, g] = qd[n, g].astype(f32).T.astype(bf16)

    for d in (1, 3, 2):
        k_d = x_at(4 - d) * 2 + core
        arrived(kv.at[k_d], "kvx", d)
        send(kv.at[k_d], kv.at[k_d], "kvc", d, core_dev)
    for d in (0, 1, 3, 2):
        arrived(kv.at[x_at(4 - d) * 2 + other], "kvc", d)

    lanes = lane_block((128, 128))
    for g in range(2):
        for a in range(4):
            q_a = jnp.where(lanes == a, qd[0, g].astype(f32), 0.0).astype(bf16)
            do_a = jnp.where(lanes == a, qd[1, g].astype(f32), 0.0).astype(bf16)
            raw_s[g * 4 + a] = nt(q_a, kv[:, 0, g].reshape(1024, 128))
            raw_p[g * 4 + a] = nt(do_a, kv[:, 1, g].reshape(1024, 128))

    for d in range(1, 8):
        arrived(bias.at[y_at(8 - d)], "ya", d)

    spot = lax.broadcasted_iota(jnp.int32, (1, 1024), 1)
    spot_c = (lax.div(spot, 256) * 8 + lax.rem(lax.div(spot, 32), 4) * 2
              + lax.rem(lax.div(spot, 128), 2))
    keep = spot_c * 32 + lax.rem(spot, 32) < length[0]
    for b in range(8):
        bias_f[:, b * 128:(b + 1) * 128] = bias[b].reshape(128, 128).astype(f32)
    dbias[...] = jnp.zeros_like(dbias)
    att[...] = jnp.zeros_like(att)
    dqkv[0] = jnp.zeros_like(dqkv[0])

    def cores_summed(g):
        arrived(dkv_c.at[g], "dkvc", g)
        for b in range(4):
            dkv_m[g, b] = (dkv_send[core, g, b].astype(f32) + dkv_c[g, b].astype(f32)).astype(bf16)
        for d in (1, 3, 2):
            send(dkv_m.at[g, x_at(d)], dkv_in.at[g, d], "dr", g * 4 + d, x_dev(d))

    for g in range(2):
        for a in range(4):
            own = lanes == a
            do_f = jnp.where(own, qd[1, g].astype(f32), 0.0)
            logits = jnp.where(keep, raw_s[g * 4 + a] + bias_f[...], NEG)
            top = jnp.max(logits, axis=-1, keepdims=True)
            expo = jnp.exp(logits - top)
            inv = 1.0 / jnp.sum(expo, axis=-1, keepdims=True)
            out = nn(expo.astype(bf16), kv[:, 1, g].reshape(1024, 128)) * inv
            out = jnp.where(own, out, 0.0)
            att[g] = att[g] + out
            delta = jnp.sum(do_f * out, axis=-1, keepdims=True)
            shares = expo * inv
            grads = shares * (raw_p[g * 4 + a] - delta)
            for b in range(8):
                dbias[b] = dbias[b] + grads[:, b * 128:(b + 1) * 128]
            grads_s[g * 4 + a] = grads.astype(bf16)
            shares_s[g * 4 + a] = shares.astype(bf16)

    for b in range(8):
        db_send[b] = dbias[b].astype(bf16)
    for d in (4, 3, 5, 2, 6, 1, 7):
        send(db_send.at[y_at(d)], db_y.at[d], "yr", d, y_dev(d))
    for d in (1, 3, 2):
        rows_d = pl.ds(pl.multiple_of(z_at(d) * 32, 32), 32)
        send(att.at[:, rows_d, :], o_in.at[z], "oz", d, z_dev(d))
    o_in[z] = att[:, z_rows, :]

    for g in range(2):
        for a in range(4):
            if (g, a) == (1, 2):
                cores_summed(0)
            grads = grads_s[g * 4 + a]
            dq = nn(grads, kv[:, 0, g].reshape(1024, 128)) * (32 ** (-0.5))
            dqkv[0, g] = jnp.where(lanes == a, dq, dqkv[0, g].astype(f32)).astype(bf16)
            part = slice(a * 32, (a + 1) * 32)
            dk = nn(qdt[0, g, part, :], grads).astype(bf16)
            dv = nn(qdt[1, g, part, :], shares_s[g * 4 + a]).astype(bf16)
            for b in range(8):
                dkv_send[b % 2, g, b // 2, 0, part, :] = dk[:, b * 128:(b + 1) * 128]
                dkv_send[b % 2, g, b // 2, 1, part, :] = dv[:, b * 128:(b + 1) * 128]
        send(dkv_send.at[other, g], dkv_c.at[g], "dkvc", g, core_dev)
    for d in (1, 3, 2):
        rows_d = pl.ds(pl.multiple_of(z_at(d) * 32, 32), 32)
        send(dqkv.at[0, :, rows_d, :], e_in.at[z, 0], "dqz", d, z_dev(d))
    e_in[z, 0] = dqkv[0, :, z_rows, :]
    cores_summed(1)

    total = dbias[y]
    for d in range(1, 8):
        arrived(db_y.at[d], "yr", d)
        total = total + db_y[d].astype(f32)
    db_s[...] = total.reshape(2, 64, 128).astype(bf16)
    turn_own(db_s.at[core], db_t.at[core], "dt", core, by_row(core))
    send(db_s.at[other], db_t.at[core], "dt", 1, by_row(other), core)

    for g in range(2):
        for d in (1, 3, 2):
            arrived(dkv_in.at[g, d], "dr", g * 4 + d)
        for n in range(2):
            total = dkv_m[g, x, n].astype(f32)
            for d in (1, 2, 3):
                total = total + dkv_in[g, d, n].astype(f32)
            dqkv[1 + n, g] = total.T.astype(bf16)
    for d in (1, 3, 2):
        rows_d = pl.ds(pl.multiple_of(z_at(d) * 32, 32), 32)
        send(dqkv.at[1:3, :, rows_d, :], e_in.at[z, 1:3], "dkvz", d, z_dev(d))
    e_in[z, 1:3] = dqkv[1:3, :, z_rows, :]

    arrived(db_t.at[0], "dt", 0)
    arrived(db_t.at[1], "dt", 1)
    for e in range(2):
        final = db_t[:, e * 32:(e + 1) * 32, :].astype(f32).reshape(64, 128)
        outs = lane_swap([final[q * 16:(q + 1) * 16] for q in range(4)])
        for b in range(4):
            db_out[e, b] = outs[b]
    for e, d in AROUND[1:]:
        send(db_out.at[lax.rem(zhi + e, 2), z_at(d)], db_in.at[zhi, z], "dbz", e * 4 + d,
             zz_dev(e, d))
    db_in[zhi, z] = db_out[zhi, z]

    for d in (1, 2, 3):
        h_d = z_at(4 - d)
        arrived(o_in.at[h_d], "oz", d)
        arrived(e_in.at[h_d, 0], "dqz", d)
    gated = []
    pres = []
    for g in range(2):
        outs = lane_swap([o_in[h, g] for h in range(4)])
        for i in range(4):
            at = slice((g * 4 + i) * 32, (g * 4 + i + 1) * 32)
            gate_t, gg_t = gate_s[at], gg_s[at]
            gated.append((gate_t * outs[i]).astype(bf16))
            pres.append((gg_t * outs[i] * gate_t * (1.0 - gate_t)).astype(bf16))
    update[...] = nn(jnp.concatenate(gated, axis=0), w_out[...]).astype(bf16).reshape(8, 32, 128)
    for d in (1, 2, 3):
        arrived(e_in.at[z_at(4 - d), 1:3], "dkvz", d)
    sides = [jnp.concatenate(pres, axis=0)]
    for n in range(3):
        tiles = []
        for g in range(2):
            tiles += lane_swap([e_in[h, n, g].astype(f32) for h in range(4)])
        sides.append(jnp.concatenate(tiles, axis=0).astype(bf16))
    grad_window = (nt(sides[1], w_query[...]) + nt(sides[2], w_key[...])
                   + nt(sides[3], w_value[...]) + nt(sides[0], w_gate[...]))
    gw[0:8] = grad_window.reshape(8, 32, 128)
    gw[8:16] = jnp.zeros((8, 32, 128), f32)

    for e, d in AROUND[1:]:
        arrived(db_in.at[lax.rem(zhi + e, 2), z_at(4 - d)], "dbz", e * 4 + d)
    flat = (db_in[0] + db_in[1]).reshape(64, 128).T
    high = flat.astype(bf16)
    rest = flat - high.astype(f32)
    mid = rest.astype(bf16)
    low = (rest - mid.astype(f32)).astype(bf16)

    def leave(i):
        part = pl.ds(i * 2, 2)
        return pltpu.make_async_copy(result_s.at[:, part], pair_grad.at[:, part], leave_sem.at[i])

    def final_step(i, carry):
        for u in range(2):
            jj = i * 2 + u
            chosen = jnp.where(row_in == jj, w_rows[...].astype(f32), 0.0).astype(bf16)
            grad = nn(high, chosen) + (nn(mid, chosen) + nn(low, chosen))
            grad = jnp.concatenate([grad[0:32] + gw[jj], grad[32:]], axis=0) * gain_v
            hat = xhat[jj]
            first = jnp.mean(grad, axis=-1, keepdims=True)
            second = jnp.mean(grad * hat, axis=-1, keepdims=True)
            result = rstd_all[jj] * (grad - first - hat * second)
            for q in range(4):
                result_s[q, jj] = result[q * 32:(q + 1) * 32]
        leave(i).start()
        return carry

    lax.fori_loop(0, 8, final_step, 0)
    for i in range(8):
        leave(i).wait()

    for copy in sent:
        copy.wait_send()

    @pl.when(jnp.logical_not(stays))
    def _():
        for copy in turned:
            copy.wait_send()


def body(pair, length, ln_gain, w_query, w_key, w_value, w_gate, w_bias, w_out, out_grad):
    vmem = pl.BlockSpec(memory_space=pltpu.VMEM)
    hbm = pl.BlockSpec(memory_space=pltpu.HBM)
    smem = pl.BlockSpec(memory_space=pltpu.SMEM)

    scratch = [
        pltpu.VMEM(pair.shape, bf16),
        *[pltpu.VMEM((128, 128), bf16) for _ in range(5)],
        pltpu.VMEM(out_grad.shape, bf16),
        pltpu.SemaphoreType.DMA((7,)),
        pltpu.VMEM((16, 128, 128), f32),
        pltpu.VMEM((16, 128, 128), f32),
        pltpu.VMEM((64, 128), bf16),
        pltpu.VMEM((256, 128), f32),
        pltpu.VMEM((256, 128), f32),
        pltpu.VMEM((4, 4, 2, 32, 128), bf16),
        pltpu.VMEM((8, 2, 2, 128, 128), bf16),
        pltpu.VMEM((2, 2, 128, 128), bf16),
        pltpu.VMEM((2, 2, 128, 128), bf16),
        pltpu.VMEM((4, 16, 128), bf16),
        pltpu.VMEM((2, 2, 4, 16, 128), bf16),
        pltpu.VMEM((8, 2, 2, 32, 128), bf16),
        pltpu.VMEM((128, 1024), f32),
        pltpu.VMEM((8, 128, 128), f32),
        pltpu.VMEM((2, 128, 128), f32),
        pltpu.VMEM((3, 2, 128, 128), bf16),
        pltpu.VMEM((8, 128, 128), bf16),
        pltpu.VMEM((8, 128, 128), bf16),
        pltpu.VMEM((2, 64, 128), bf16),
        pltpu.VMEM((2, 64, 128), bf16),
        pltpu.VMEM((2, 4, 16, 128), f32),
        pltpu.VMEM((2, 4, 16, 128), f32),
        pltpu.VMEM((2, 2, 4, 2, 128, 128), bf16),
        pltpu.VMEM((2, 4, 2, 128, 128), bf16),
        pltpu.VMEM((2, 4, 2, 128, 128), bf16),
        pltpu.VMEM((2, 4, 2, 128, 128), bf16),
        pltpu.VMEM((4, 3, 2, 32, 128), bf16),
        pltpu.VMEM((4, 2, 32, 128), f32),
        pltpu.VMEM((16, 32, 128), f32),
        pltpu.VMEM((8, 128, 1024), f32),
        pltpu.VMEM((8, 128, 1024), f32),
        pltpu.VMEM((8, 128, 1024), bf16),
        pltpu.VMEM((8, 128, 1024), bf16),
        pltpu.VMEM((4, 16, 32, 128), f32),
        pltpu.SemaphoreType.DMA((8,)),
    ]
    for _, n in COPIES:
        scratch += [pltpu.SemaphoreType.DMA((n,)), pltpu.SemaphoreType.DMA((n,))]
    call = pl.pallas_call(
        kernel,
        out_shape=(
            jax.ShapeDtypeStruct(out_grad.shape, bf16),
            jax.ShapeDtypeStruct((4, 16, 32, 128), f32),
        ),
        in_specs=[hbm, smem, vmem, hbm, hbm, hbm, hbm, vmem, hbm, hbm],
        out_specs=(vmem, hbm),
        scratch_shapes=scratch,
        compiler_params=pltpu.CompilerParams(
            collective_id=0, has_side_effects=True, vmem_limit_bytes=63 * 1024 * 1024
        ),
    )
    update, pair_grad = call(
        pair, length, ln_gain.reshape(1, 128), w_query, w_key, w_value, w_gate, w_bias.T, w_out,
        out_grad,
    )
    return update, pair_grad.reshape(pair.shape)


def solution(mesh):
    tiled = P("rows", "cols", None)
    placed = (tiled, P(), P(), P(), P(), P(), P(), P(), P(), tiled)
    return jax.shard_map(
        body, mesh=mesh, in_specs=placed, out_specs=(tiled, tiled), check_vma=False
    )
```

```python
import jax
import jax.numpy as jnp
from jax import lax
from jax.experimental import pallas as pl
from jax.experimental.pallas import tpu as pltpu
from jax.sharding import PartitionSpec as P

EPS = 1e-05
NEG = -1000000000.0
MESH = pl.DeviceIdType.MESH
f32 = jnp.float32
bf16 = jnp.bfloat16
COPIES = (
    ("kvz", 4), ("qdz", 4), ("bt", 16), ("kvx", 4), ("kvc", 4), ("ya", 8), ("dkvc", 2), ("dr", 8),
    ("yr", 8), ("dt", 2), ("dbz", 8), ("oz", 4), ("dqz", 4), ("dkvz", 4),
)

AROUND = ((0, 0), (0, 1), (0, 3), (0, 2), (1, 0), (1, 1), (1, 3), (1, 2))


def nn(left, right):
    return lax.dot_general(left, right, (((1,), (0,)), ((), ())), preferred_element_type=f32)


def nt(left, right):
    return lax.dot_general(left, right, (((1,), (1,)), ((), ())), preferred_element_type=f32)


def lane_block(shape):
    return lax.shift_right_logical(lax.broadcasted_iota(jnp.int32, shape, len(shape) - 1), 5)


def lane_swap(tiles):
    block = lane_block(tiles[0].shape)
    outs = []
    for i in range(4):
        acc = None
        for b in range(4):
            shift = (32 * (b - i)) % 128
            moved = tiles[b] if shift == 0 else pltpu.roll(tiles[b], shift, 1)
            acc = moved if acc is None else jnp.where(block == b, moved, acc)
        outs.append(acc)
    return outs


def remote(src, dst, send_sem, recv_sem, device):
    return pltpu.make_async_remote_copy(
        src_ref=src, dst_ref=dst, send_sem=send_sem, recv_sem=recv_sem,
        device_id=device, device_id_type=MESH,
    )


def kernel(
    pair_h, length, gain, w_query_h, w_key_h, w_value_h, w_gate_h, w_bias, w_out_h, out_grad_h,
    update, pair_grad,
    pair, w_query, w_key, w_value, w_gate, w_out, out_grad, load_sem, xhat, rstd_all, w_rows, gate_s, gg_s, zsend, kv, qd, qdt, bsend, brecv, bias, bias_f,
    dbias, att, dqkv, db_send, db_y, db_s, db_t, db_out, db_in, dkv_send, dkv_c, dkv_m, dkv_in,
    e_in, o_in, gw, raw_s, raw_p, grads_s, shares_s, result_s, leave_sem,
    update_s,
    *sems,
):
    sem = {name: sems[2 * n:2 * n + 2] for n, (name, _) in enumerate(COPIES)}
    row = lax.axis_index("rows")
    col = lax.axis_index("cols")
    y, zhi = lax.div(row, 2), lax.rem(row, 2)
    x, z, core = lax.div(col, 8), lax.rem(lax.div(col, 2), 4), lax.rem(col, 2)
    blk = x * 2 + core
    other = 1 - core

    def device(row_, x_, z_, core_):
        return {"rows": row_, "cols": x_ * 8 + z_ * 2 + core_}

    def z_at(d):
        return lax.rem(z + d, 4)

    def z_dev(d):
        return device(row, x, z_at(d), core)

    def x_at(d):
        return lax.rem(x + d, 4)

    def x_dev(d):
        return device(row, x_at(d), z, core)

    def y_at(d):
        return lax.rem(y + d, 8)

    def y_dev(d):
        return device(y_at(d) * 2 + zhi, x, z, core)

    def zz_dev(e, d):
        return device(y * 2 + lax.rem(zhi + e, 2), x, z_at(d), core)

    def by_column(e, d, c):
        return device(blk * 2 + lax.rem(zhi + e, 2), lax.div(y, 2), z_at(d), c)

    def by_row_all(e, d, s):
        return device(
            (x * 2 + s) * 2 + lax.rem(zhi + e, 2), lax.div(y, 2), z_at(d), lax.rem(y, 2))

    def by_row(s):
        return device((x * 2 + s) * 2 + zhi, lax.div(y, 2), z, lax.rem(y, 2))

    core_dev = device(row, x, z, other)
    stays = blk == y

    sent = []
    turned = []

    def send(src, dst, name, n, dev, at=None):
        copy = remote(src, dst, sem[name][0].at[n], sem[name][1].at[n if at is None else at], dev)
        copy.start()
        sent.append(copy)

    def turn_own(src, dst, name, at, dev):
        away = remote(src, dst, sem[name][0].at[0], sem[name][1].at[at], dev)
        here = pltpu.make_async_copy(src, dst, sem[name][1].at[at])

        @pl.when(stays)
        def _():
            here.start()

        @pl.when(jnp.logical_not(stays))
        def _():
            away.start()

        turned.append(away)

    def arrived(slot, name, n):
        remote(slot, slot, sem[name][0].at[n], sem[name][1].at[n], core_dev).wait_recv()

    barrier = pltpu.get_barrier_semaphore()
    turns = [(e, d, other) for e in range(2) for d in range(4)]
    turns += [(e, d, core) for e in range(2) for d in range(4) if (e, d) != (0, 0)]
    partners = [by_row_all(*turn) for turn in reversed(turns)] + [by_column(0, 0, other)]
    partners += [y_dev(d) for d in (4, 3, 5, 2, 6, 1, 7)] + [x_dev(d) for d in (2, 1, 3)]
    partners += [zz_dev(e, d) for e, d in reversed(AROUND[1:])] + [core_dev]

    def greet(dev):
        pl.semaphore_signal(barrier, inc=1, device_id=dev, device_id_type=MESH)

    @pl.when(jnp.logical_not(stays))
    def _():
        greet(by_column(0, 0, core))
        greet(by_row(core))

    for dev in partners:
        greet(dev)

    loads = [
        pltpu.make_async_copy(src, dst, load_sem.at[n])
        for n, (src, dst) in enumerate((
            (pair_h, pair), (w_query_h, w_query), (w_key_h, w_key), (w_value_h, w_value),
            (w_gate_h, w_gate), (w_out_h, w_out), (out_grad_h, out_grad)))
    ]
    for copy in loads:
        copy.start()

    gain_v = gain[...]
    for copy in loads:
        copy.wait()

    def norm(values):
        average = jnp.mean(values, axis=-1, keepdims=True)
        centred = values - average
        variance = jnp.mean(centred * centred, axis=-1, keepdims=True)
        rstd = lax.rsqrt(variance + EPS)
        return centred * rstd, rstd, centred

    win = pair[0:8].reshape(256, 128).astype(f32)
    hat, _, _ = norm(win)
    window = (hat * gain_v).astype(bf16)
    query = (nn(window, w_query[...]) * (32 ** (-0.5))).astype(bf16).astype(f32)
    keys = nn(window, w_key[...]).astype(bf16).astype(f32)
    vals = nn(window, w_value[...]).astype(bf16).astype(f32)
    gate = jax.nn.sigmoid(nn(window, w_gate[...])).astype(bf16).astype(f32)
    gg = nt(out_grad[...].reshape(256, 128), w_out[...])
    ga = (gg * gate).astype(bf16).astype(f32)
    gate_s[...] = gate
    gg_s[...] = gg
    for n, array in enumerate((keys, vals, query, ga)):
        for g in range(2):
            outs = lane_swap([array[(g * 4 + b) * 32:(g * 4 + b + 1) * 32] for b in range(4)])
            for h in range(4):
                zsend[h, n, g] = outs[h].astype(bf16)

    pick = lax.broadcasted_iota(jnp.int32, (64, 4), 0) // 16 == lax.broadcasted_iota(
        jnp.int32, (64, 4), 1)
    w_rows[...] = nn(pick.astype(bf16), w_bias[...]).astype(bf16)
    row_in = lax.rem(lax.broadcasted_iota(jnp.int32, (64, 128), 0), 16)

    def tile_step(i, acc):
        for u in range(4):
            jj = i * 4 + u
            tokens = jnp.concatenate([pair[q * 16 + jj] for q in range(4)], axis=0).astype(f32)
            hat, rstd, _ = norm(tokens)
            xhat[jj] = hat
            rstd_all[jj] = jnp.broadcast_to(rstd, (128, 128))
            normed = (hat * gain_v).astype(bf16)
            chosen = jnp.where(row_in == jj, w_rows[...].astype(f32), 0.0).astype(bf16)
            acc = acc + nt(chosen, normed)
        return acc

    tile_bias = lax.fori_loop(0, 4, tile_step, jnp.zeros((64, 128), f32))
    bsend[...] = tile_bias.astype(bf16).reshape(4, 16, 128)
    pl.semaphore_wait(barrier, len(partners) + jnp.where(stays, 0, 2))

    odd = lax.rem(y, 2)
    turn_own(bsend.at[z], brecv.at[odd, zhi, z], "bt", odd * 8, by_column(0, 0, core))
    for n, c in enumerate((core, other)):
        for e, d in AROUND:
            if (n, e, d) != (0, 0, 0):
                send(bsend.at[z_at(d)], brecv.at[odd, zhi, z], "bt", n * 8 + e * 4 + d,
                     by_column(e, d, c), odd * 8 + e * 4 + d)
    z_rows = pl.ds(pl.multiple_of(z * 32, 32), 32)
    for d in (1, 3, 2):
        send(zsend.at[z_at(d), 0:2], kv.at[blk, :, :, z_rows, :], "kvz", d, z_dev(d))
    kv[blk, :, :, z_rows, :] = zsend[z, 0:2]
    qd[:, :, z_rows, :] = zsend[z, 2:4]

    for d in (1, 3, 2):
        send(zsend.at[z_at(d), 2:4], qd.at[:, :, z_rows, :], "qdz", d, z_dev(d))

    for d in (1, 2, 3):
        rows_d = pl.ds(pl.multiple_of(z_at(4 - d) * 32, 32), 32)
        arrived(kv.at[blk, :, :, rows_d, :], "kvz", d)
    for d in (1, 3, 2):
        send(kv.at[blk], kv.at[blk], "kvx", d, x_dev(d))
    send(kv.at[blk], kv.at[blk], "kvc", 0, core_dev)

    for n in range(2):
        for e, d in AROUND:
            arrived(brecv.at[n, lax.rem(zhi + e, 2), z_at(4 - d)], "bt", n * 8 + e * 4 + d)
    for n in range(2):
        for e in range(2):
            outs = lane_swap([brecv[n, e, b].astype(f32) for b in range(4)])
            bias[y, n, e, 0:16] = jnp.where(core == 0, outs[0], outs[2]).astype(bf16)
            bias[y, n, e, 16:32] = jnp.where(core == 0, outs[1], outs[3]).astype(bf16)
    for d in (4, 3, 5, 2, 6, 1, 7):
        send(bias.at[y], bias.at[y], "ya", d, y_dev(d))

    for d in (1, 2, 3):
        rows_d = pl.ds(pl.multiple_of(z_at(4 - d) * 32, 32), 32)
        arrived(qd.at[:, :, rows_d, :], "qdz", d)
    for n in range(2):
        for g in range(2):
            qdt[n, g] = qd[n, g].astype(f32).T.astype(bf16)

    for d in (1, 3, 2):
        k_d = x_at(4 - d) * 2 + core
        arrived(kv.at[k_d], "kvx", d)
        send(kv.at[k_d], kv.at[k_d], "kvc", d, core_dev)
    for d in (0, 1, 3, 2):
        arrived(kv.at[x_at(4 - d) * 2 + other], "kvc", d)

    lanes = lane_block((128, 128))
    for g in range(2):
        for a in range(4):
            q_a = jnp.where(lanes == a, qd[0, g].astype(f32), 0.0).astype(bf16)
            do_a = jnp.where(lanes == a, qd[1, g].astype(f32), 0.0).astype(bf16)
            raw_s[g * 4 + a] = nt(q_a, kv[:, 0, g].reshape(1024, 128))
            raw_p[g * 4 + a] = nt(do_a, kv[:, 1, g].reshape(1024, 128))

    for d in range(1, 8):
        arrived(bias.at[y_at(8 - d)], "ya", d)

    spot = lax.broadcasted_iota(jnp.int32, (1, 1024), 1)
    spot_c = (lax.div(spot, 256) * 8 + lax.rem(lax.div(spot, 32), 4) * 2
              + lax.rem(lax.div(spot, 128), 2))
    keep = spot_c * 32 + lax.rem(spot, 32) < length[0]
    for b in range(8):
        bias_f[:, b * 128:(b + 1) * 128] = bias[b].reshape(128, 128).astype(f32)
    dbias[...] = jnp.zeros_like(dbias)
    att[...] = jnp.zeros_like(att)
    dqkv[0] = jnp.zeros_like(dqkv[0])

    def cores_summed(g):
        arrived(dkv_c.at[g], "dkvc", g)
        for b in range(4):
            dkv_m[g, b] = (dkv_send[core, g, b].astype(f32) + dkv_c[g, b].astype(f32)).astype(bf16)
        for d in (1, 3, 2):
            send(dkv_m.at[g, x_at(d)], dkv_in.at[g, d], "dr", g * 4 + d, x_dev(d))

    for g in range(2):
        for a in range(4):
            own = lanes == a
            do_f = jnp.where(own, qd[1, g].astype(f32), 0.0)
            logits = jnp.where(keep, raw_s[g * 4 + a] + bias_f[...], NEG)
            top = jnp.max(logits, axis=-1, keepdims=True)
            expo = jnp.exp(logits - top)
            inv = 1.0 / jnp.sum(expo, axis=-1, keepdims=True)
            out = nn(expo.astype(bf16), kv[:, 1, g].reshape(1024, 128)) * inv
            out = jnp.where(own, out, 0.0)
            att[g] = att[g] + out
            delta = jnp.sum(do_f * out, axis=-1, keepdims=True)
            shares = expo * inv
            grads = shares * (raw_p[g * 4 + a] - delta)
            for b in range(8):
                dbias[b] = dbias[b] + grads[:, b * 128:(b + 1) * 128]
            grads_s[g * 4 + a] = grads.astype(bf16)
            shares_s[g * 4 + a] = shares.astype(bf16)

    for b in range(8):
        db_send[b] = dbias[b].astype(bf16)
    for d in (4, 3, 5, 2, 6, 1, 7):
        send(db_send.at[y_at(d)], db_y.at[d], "yr", d, y_dev(d))
    for d in (1, 3, 2):
        rows_d = pl.ds(pl.multiple_of(z_at(d) * 32, 32), 32)
        send(att.at[:, rows_d, :], o_in.at[z], "oz", d, z_dev(d))
    o_in[z] = att[:, z_rows, :]

    for g in range(2):
        for a in range(4):
            if (g, a) == (1, 2):
                cores_summed(0)
            grads = grads_s[g * 4 + a]
            part = slice(a * 32, (a + 1) * 32)
            dk = nn(qdt[0, g, part, :], grads).astype(bf16)
            dv = nn(qdt[1, g, part, :], shares_s[g * 4 + a]).astype(bf16)
            for b in range(8):
                dkv_send[b % 2, g, b // 2, 0, part, :] = dk[:, b * 128:(b + 1) * 128]
                dkv_send[b % 2, g, b // 2, 1, part, :] = dv[:, b * 128:(b + 1) * 128]
        send(dkv_send.at[other, g], dkv_c.at[g], "dkvc", g, core_dev)
    for g in range(2):
        for a in range(4):
            dq = nn(grads_s[g * 4 + a], kv[:, 0, g].reshape(1024, 128)) * (32 ** (-0.5))
            dqkv[0, g] = jnp.where(lanes == a, dq, dqkv[0, g].astype(f32)).astype(bf16)
    for d in (1, 3, 2):
        rows_d = pl.ds(pl.multiple_of(z_at(d) * 32, 32), 32)
        send(dqkv.at[0, :, rows_d, :], e_in.at[z, 0], "dqz", d, z_dev(d))
    e_in[z, 0] = dqkv[0, :, z_rows, :]
    cores_summed(1)

    total = dbias[y]
    for d in range(1, 8):
        arrived(db_y.at[d], "yr", d)
        total = total + db_y[d].astype(f32)
    db_s[...] = total.reshape(2, 64, 128).astype(bf16)
    turn_own(db_s.at[core], db_t.at[core], "dt", core, by_row(core))
    send(db_s.at[other], db_t.at[core], "dt", 1, by_row(other), core)

    for g in range(2):
        for d in (1, 3, 2):
            arrived(dkv_in.at[g, d], "dr", g * 4 + d)
        for n in range(2):
            total = dkv_m[g, x, n].astype(f32)
            for d in (1, 2, 3):
                total = total + dkv_in[g, d, n].astype(f32)
            dqkv[1 + n, g] = total.T.astype(bf16)
    for d in (1, 3, 2):
        rows_d = pl.ds(pl.multiple_of(z_at(d) * 32, 32), 32)
        send(dqkv.at[1:3, :, rows_d, :], e_in.at[z, 1:3], "dkvz", d, z_dev(d))
    e_in[z, 1:3] = dqkv[1:3, :, z_rows, :]

    arrived(db_t.at[0], "dt", 0)
    arrived(db_t.at[1], "dt", 1)
    for e in range(2):
        final = db_t[:, e * 32:(e + 1) * 32, :].astype(f32).reshape(64, 128)
        outs = lane_swap([final[q * 16:(q + 1) * 16] for q in range(4)])
        for b in range(4):
            db_out[e, b] = outs[b]
    for e, d in AROUND[1:]:
        send(db_out.at[lax.rem(zhi + e, 2), z_at(d)], db_in.at[zhi, z], "dbz", e * 4 + d,
             zz_dev(e, d))
    db_in[zhi, z] = db_out[zhi, z]

    for d in (1, 2, 3):
        h_d = z_at(4 - d)
        arrived(o_in.at[h_d], "oz", d)
        arrived(e_in.at[h_d, 0], "dqz", d)
    gated = []
    pres = []
    for g in range(2):
        outs = lane_swap([o_in[h, g] for h in range(4)])
        for i in range(4):
            at = slice((g * 4 + i) * 32, (g * 4 + i + 1) * 32)
            gate_t, gg_t = gate_s[at], gg_s[at]
            gated.append((gate_t * outs[i]).astype(bf16))
            pres.append((gg_t * outs[i] * gate_t * (1.0 - gate_t)).astype(bf16))
    update_s[...] = nn(jnp.concatenate(gated, axis=0), w_out[...]).astype(bf16).reshape(8, 32, 128)
    update_out = pltpu.make_async_copy(update_s, update, leave_sem.at[4])
    update_out.start()
    for d in (1, 2, 3):
        arrived(e_in.at[z_at(4 - d), 1:3], "dkvz", d)
    sides = [jnp.concatenate(pres, axis=0)]
    for n in range(3):
        tiles = []
        for g in range(2):
            tiles += lane_swap([e_in[h, n, g].astype(f32) for h in range(4)])
        sides.append(jnp.concatenate(tiles, axis=0).astype(bf16))
    grad_window = (nt(sides[1], w_query[...]) + nt(sides[2], w_key[...])
                   + nt(sides[3], w_value[...]) + nt(sides[0], w_gate[...]))
    gw[0:8] = grad_window.reshape(8, 32, 128)
    gw[8:16] = jnp.zeros((8, 32, 128), f32)

    for copy in sent[:-7]:
        copy.wait_send()
    for e, d in AROUND[1:]:
        arrived(db_in.at[lax.rem(zhi + e, 2), z_at(4 - d)], "dbz", e * 4 + d)
    flat = (db_in[0] + db_in[1]).reshape(64, 128).T
    high = flat.astype(bf16)
    rest = flat - high.astype(f32)
    mid = rest.astype(bf16)
    low = (rest - mid.astype(f32)).astype(bf16)

    def leave(i):
        part = pl.ds(i * 4, 4)
        return pltpu.make_async_copy(result_s.at[:, part], pair_grad.at[:, part], leave_sem.at[i])

    def final_step(i, carry):
        for u in range(4):
            jj = i * 4 + u
            chosen = jnp.where(row_in == jj, w_rows[...].astype(f32), 0.0).astype(bf16)
            grad = nn(high, chosen) + (nn(mid, chosen) + nn(low, chosen))
            grad = jnp.concatenate([grad[0:32] + gw[jj], grad[32:]], axis=0) * gain_v
            hat = xhat[jj]
            first = jnp.mean(grad, axis=-1, keepdims=True)
            second = jnp.mean(grad * hat, axis=-1, keepdims=True)
            result = rstd_all[jj] * (grad - first - hat * second)
            for q in range(4):
                result_s[q, jj] = result[q * 32:(q + 1) * 32]
        leave(i).start()
        return carry

    lax.fori_loop(0, 4, final_step, 0)
    for i in range(4):
        leave(i).wait()
    update_out.wait()

    for copy in sent[-7:]:
        copy.wait_send()

    @pl.when(jnp.logical_not(stays))
    def _():
        for copy in turned:
            copy.wait_send()


def body(pair, length, ln_gain, w_query, w_key, w_value, w_gate, w_bias, w_out, out_grad):
    vmem = pl.BlockSpec(memory_space=pltpu.VMEM)
    hbm = pl.BlockSpec(memory_space=pltpu.HBM)
    smem = pl.BlockSpec(memory_space=pltpu.SMEM)

    scratch = [
        pltpu.VMEM(pair.shape, bf16),
        *[pltpu.VMEM((128, 128), bf16) for _ in range(5)],
        pltpu.VMEM(out_grad.shape, bf16),
        pltpu.SemaphoreType.DMA((7,)),
        pltpu.VMEM((16, 128, 128), f32),
        pltpu.VMEM((16, 128, 128), f32),
        pltpu.VMEM((64, 128), bf16),
        pltpu.VMEM((256, 128), f32),
        pltpu.VMEM((256, 128), f32),
        pltpu.VMEM((4, 4, 2, 32, 128), bf16),
        pltpu.VMEM((8, 2, 2, 128, 128), bf16),
        pltpu.VMEM((2, 2, 128, 128), bf16),
        pltpu.VMEM((2, 2, 128, 128), bf16),
        pltpu.VMEM((4, 16, 128), bf16),
        pltpu.VMEM((2, 2, 4, 16, 128), bf16),
        pltpu.VMEM((8, 2, 2, 32, 128), bf16),
        pltpu.VMEM((128, 1024), f32),
        pltpu.VMEM((8, 128, 128), f32),
        pltpu.VMEM((2, 128, 128), f32),
        pltpu.VMEM((3, 2, 128, 128), bf16),
        pltpu.VMEM((8, 128, 128), bf16),
        pltpu.VMEM((8, 128, 128), bf16),
        pltpu.VMEM((2, 64, 128), bf16),
        pltpu.VMEM((2, 64, 128), bf16),
        pltpu.VMEM((2, 4, 16, 128), f32),
        pltpu.VMEM((2, 4, 16, 128), f32),
        pltpu.VMEM((2, 2, 4, 2, 128, 128), bf16),
        pltpu.VMEM((2, 4, 2, 128, 128), bf16),
        pltpu.VMEM((2, 4, 2, 128, 128), bf16),
        pltpu.VMEM((2, 4, 2, 128, 128), bf16),
        pltpu.VMEM((4, 3, 2, 32, 128), bf16),
        pltpu.VMEM((4, 2, 32, 128), f32),
        pltpu.VMEM((16, 32, 128), f32),
        pltpu.VMEM((8, 128, 1024), f32),
        pltpu.VMEM((8, 128, 1024), f32),
        pltpu.VMEM((8, 128, 1024), bf16),
        pltpu.VMEM((8, 128, 1024), bf16),
        pltpu.VMEM((4, 16, 32, 128), f32),
        pltpu.SemaphoreType.DMA((5,)),
        pltpu.VMEM(out_grad.shape, bf16),
    ]
    for _, n in COPIES:
        scratch += [pltpu.SemaphoreType.DMA((n,)), pltpu.SemaphoreType.DMA((n,))]
    call = pl.pallas_call(
        kernel,
        out_shape=(
            jax.ShapeDtypeStruct(out_grad.shape, bf16),
            jax.ShapeDtypeStruct((4, 16, 32, 128), f32),
        ),
        in_specs=[hbm, smem, vmem, hbm, hbm, hbm, hbm, vmem, hbm, hbm],
        out_specs=(hbm, hbm),
        scratch_shapes=scratch,
        compiler_params=pltpu.CompilerParams(
            collective_id=0, has_side_effects=True, vmem_limit_bytes=63 * 1024 * 1024
        ),
    )
    update, pair_grad = call(
        pair, length, ln_gain.reshape(1, 128), w_query, w_key, w_value, w_gate, w_bias.T, w_out,
        out_grad,
    )
    return update, pair_grad.reshape(pair.shape)


def solution(mesh):
    tiled = P("rows", "cols", None)
    placed = (tiled, P(), P(), P(), P(), P(), P(), P(), P(), tiled)
    return jax.shard_map(
        body, mesh=mesh, in_specs=placed, out_specs=(tiled, tiled), check_vma=False
    )
```

```python
import jax
import jax.numpy as jnp
from jax import lax
from jax.experimental import pallas as pl
from jax.experimental.pallas import tpu as pltpu
from jax.sharding import PartitionSpec as P

EPS = 1e-05
NEG = -1000000000.0
MESH = pl.DeviceIdType.MESH
f32 = jnp.float32
bf16 = jnp.bfloat16
COPIES = (
    ("kvz", 4), ("qdz", 4), ("bt", 16), ("kvx", 4), ("kvc", 4), ("ya", 8), ("dkvc", 2), ("dr", 8),
    ("yr", 8), ("dt", 2), ("dbz", 8), ("oz", 4), ("dqz", 4), ("dkvz", 4),
)

AROUND = ((0, 0), (0, 1), (0, 3), (0, 2), (1, 0), (1, 1), (1, 3), (1, 2))


def nn(left, right):
    return lax.dot_general(left, right, (((1,), (0,)), ((), ())), preferred_element_type=f32)


def nt(left, right):
    return lax.dot_general(left, right, (((1,), (1,)), ((), ())), preferred_element_type=f32)


def lane_block(shape):
    return lax.shift_right_logical(lax.broadcasted_iota(jnp.int32, shape, len(shape) - 1), 5)


def lane_swap(tiles):
    block = lane_block(tiles[0].shape)
    outs = []
    for i in range(4):
        acc = None
        for b in range(4):
            shift = (32 * (b - i)) % 128
            moved = tiles[b] if shift == 0 else pltpu.roll(tiles[b], shift, 1)
            acc = moved if acc is None else jnp.where(block == b, moved, acc)
        outs.append(acc)
    return outs


def remote(src, dst, send_sem, recv_sem, device):
    return pltpu.make_async_remote_copy(
        src_ref=src, dst_ref=dst, send_sem=send_sem, recv_sem=recv_sem,
        device_id=device, device_id_type=MESH,
    )


def kernel(
    pair_h, length, gain, w_query_h, w_key_h, w_value_h, w_gate_h, w_bias, w_out_h, out_grad_h,
    update, pair_grad,
    pair, w_query, w_key, w_value, w_gate, w_out, out_grad, load_sem, xhat, rstd_all, w_rows, gate_s, gg_s, zsend, kv, qd, qdt, bsend, brecv, bias, bias_f,
    dbias, att, dqkv, db_send, db_y, db_s, db_t, db_out, db_in, dkv_send, dkv_c, dkv_m, dkv_in,
    e_in, o_in, gw, raw_s, raw_p, grads_s, shares_s, result_s, leave_sem,
    update_s,
    *sems,
):
    sem = {name: sems[2 * n:2 * n + 2] for n, (name, _) in enumerate(COPIES)}
    row = lax.axis_index("rows")
    col = lax.axis_index("cols")
    y, zhi = lax.div(row, 2), lax.rem(row, 2)
    x, z, core = lax.div(col, 8), lax.rem(lax.div(col, 2), 4), lax.rem(col, 2)
    blk = x * 2 + core
    other = 1 - core

    def device(row_, x_, z_, core_):
        return {"rows": row_, "cols": x_ * 8 + z_ * 2 + core_}

    def z_at(d):
        return lax.rem(z + d, 4)

    def z_dev(d):
        return device(row, x, z_at(d), core)

    def x_at(d):
        return lax.rem(x + d, 4)

    def x_dev(d):
        return device(row, x_at(d), z, core)

    def y_at(d):
        return lax.rem(y + d, 8)

    def y_dev(d):
        return device(y_at(d) * 2 + zhi, x, z, core)

    def zz_dev(e, d):
        return device(y * 2 + lax.rem(zhi + e, 2), x, z_at(d), core)

    def by_column(e, d, c):
        return device(blk * 2 + lax.rem(zhi + e, 2), lax.div(y, 2), z_at(d), c)

    def by_row_all(e, d, s):
        return device(
            (x * 2 + s) * 2 + lax.rem(zhi + e, 2), lax.div(y, 2), z_at(d), lax.rem(y, 2))

    def by_row(s):
        return device((x * 2 + s) * 2 + zhi, lax.div(y, 2), z, lax.rem(y, 2))

    core_dev = device(row, x, z, other)
    stays = blk == y

    sent = []
    turned = []

    def send(src, dst, name, n, dev, at=None):
        copy = remote(src, dst, sem[name][0].at[n], sem[name][1].at[n if at is None else at], dev)
        copy.start()
        sent.append(copy)

    def turn_own(src, dst, name, at, dev):
        away = remote(src, dst, sem[name][0].at[0], sem[name][1].at[at], dev)
        here = pltpu.make_async_copy(src, dst, sem[name][1].at[at])

        @pl.when(stays)
        def _():
            here.start()

        @pl.when(jnp.logical_not(stays))
        def _():
            away.start()

        turned.append(away)

    def arrived(slot, name, n):
        remote(slot, slot, sem[name][0].at[n], sem[name][1].at[n], core_dev).wait_recv()

    barrier = pltpu.get_barrier_semaphore()
    turns = [(e, d, other) for e in range(2) for d in range(4)]
    turns += [(e, d, core) for e in range(2) for d in range(4) if (e, d) != (0, 0)]
    partners = [by_row_all(*turn) for turn in reversed(turns)] + [by_column(0, 0, other)]
    partners += [y_dev(d) for d in (4, 3, 5, 2, 6, 1, 7)] + [x_dev(d) for d in (2, 1, 3)]
    partners += [zz_dev(e, d) for e, d in reversed(AROUND[1:])] + [core_dev]

    def greet(dev):
        pl.semaphore_signal(barrier, inc=1, device_id=dev, device_id_type=MESH)

    @pl.when(jnp.logical_not(stays))
    def _():
        greet(by_column(0, 0, core))
        greet(by_row(core))

    for dev in partners:
        greet(dev)

    loads = [
        pltpu.make_async_copy(src, dst, load_sem.at[n])
        for n, (src, dst) in enumerate((
            (pair_h, pair), (w_query_h, w_query), (w_key_h, w_key), (w_value_h, w_value),
            (w_gate_h, w_gate), (w_out_h, w_out), (out_grad_h, out_grad)))
    ]
    for copy in loads:
        copy.start()

    gain_v = gain[...]
    for copy in loads:
        copy.wait()

    def norm(values):
        average = jnp.mean(values, axis=-1, keepdims=True)
        centred = values - average
        variance = jnp.mean(centred * centred, axis=-1, keepdims=True)
        rstd = lax.rsqrt(variance + EPS)
        return centred * rstd, rstd, centred

    win = pair[0:8].reshape(256, 128).astype(f32)
    hat, _, _ = norm(win)
    window = (hat * gain_v).astype(bf16)
    query = (nn(window, w_query[...]) * (32 ** (-0.5))).astype(bf16).astype(f32)
    keys = nn(window, w_key[...]).astype(bf16).astype(f32)
    vals = nn(window, w_value[...]).astype(bf16).astype(f32)
    gate = jax.nn.sigmoid(nn(window, w_gate[...])).astype(bf16).astype(f32)
    gg = nt(out_grad[...].reshape(256, 128), w_out[...])
    ga = (gg * gate).astype(bf16).astype(f32)
    gate_s[...] = gate
    gg_s[...] = gg
    for n, array in enumerate((keys, vals, query, ga)):
        for g in range(2):
            outs = lane_swap([array[(g * 4 + b) * 32:(g * 4 + b + 1) * 32] for b in range(4)])
            for h in range(4):
                zsend[h, n, g] = outs[h].astype(bf16)

    pick = lax.broadcasted_iota(jnp.int32, (64, 4), 0) // 16 == lax.broadcasted_iota(
        jnp.int32, (64, 4), 1)
    w_rows[...] = nn(pick.astype(bf16), w_bias[...]).astype(bf16)
    row_in = lax.rem(lax.broadcasted_iota(jnp.int32, (64, 128), 0), 16)

    def tile_step(i, acc):
        for u in range(4):
            jj = i * 4 + u
            tokens = jnp.concatenate([pair[q * 16 + jj] for q in range(4)], axis=0).astype(f32)
            hat, rstd, _ = norm(tokens)
            xhat[jj] = hat
            rstd_all[jj] = jnp.broadcast_to(rstd, (128, 128))
            normed = (hat * gain_v).astype(bf16)
            chosen = jnp.where(row_in == jj, w_rows[...].astype(f32), 0.0).astype(bf16)
            acc = acc + nt(chosen, normed)
        return acc

    tile_bias = lax.fori_loop(0, 4, tile_step, jnp.zeros((64, 128), f32))
    bsend[...] = tile_bias.astype(bf16).reshape(4, 16, 128)
    pl.semaphore_wait(barrier, len(partners) + jnp.where(stays, 0, 2))

    odd = lax.rem(y, 2)
    turn_own(bsend.at[z], brecv.at[odd, zhi, z], "bt", odd * 8, by_column(0, 0, core))
    for n, c in enumerate((core, other)):
        for e, d in AROUND:
            if (n, e, d) != (0, 0, 0):
                send(bsend.at[z_at(d)], brecv.at[odd, zhi, z], "bt", n * 8 + e * 4 + d,
                     by_column(e, d, c), odd * 8 + e * 4 + d)
    z_rows = pl.ds(pl.multiple_of(z * 32, 32), 32)
    for d in (1, 3, 2):
        send(zsend.at[z_at(d), 0:2], kv.at[blk, :, :, z_rows, :], "kvz", d, z_dev(d))
    kv[blk, :, :, z_rows, :] = zsend[z, 0:2]
    qd[:, :, z_rows, :] = zsend[z, 2:4]

    for d in (1, 3, 2):
        send(zsend.at[z_at(d), 2:4], qd.at[:, :, z_rows, :], "qdz", d, z_dev(d))

    for d in (1, 2, 3):
        rows_d = pl.ds(pl.multiple_of(z_at(4 - d) * 32, 32), 32)
        arrived(kv.at[blk, :, :, rows_d, :], "kvz", d)
    for d in (1, 3, 2):
        send(kv.at[blk], kv.at[blk], "kvx", d, x_dev(d))
    send(kv.at[blk], kv.at[blk], "kvc", 0, core_dev)

    for n in range(2):
        for e, d in AROUND:
            arrived(brecv.at[n, lax.rem(zhi + e, 2), z_at(4 - d)], "bt", n * 8 + e * 4 + d)
    for n in range(2):
        for e in range(2):
            outs = lane_swap([brecv[n, e, b].astype(f32) for b in range(4)])
            bias[y, n, e, 0:16] = jnp.where(core == 0, outs[0], outs[2]).astype(bf16)
            bias[y, n, e, 16:32] = jnp.where(core == 0, outs[1], outs[3]).astype(bf16)
    for d in (4, 3, 5, 2, 6, 1, 7):
        send(bias.at[y], bias.at[y], "ya", d, y_dev(d))

    for d in (1, 2, 3):
        rows_d = pl.ds(pl.multiple_of(z_at(4 - d) * 32, 32), 32)
        arrived(qd.at[:, :, rows_d, :], "qdz", d)
    for n in range(2):
        for g in range(2):
            qdt[n, g] = qd[n, g].astype(f32).T.astype(bf16)

    for d in (1, 3, 2):
        k_d = x_at(4 - d) * 2 + core
        arrived(kv.at[k_d], "kvx", d)
        send(kv.at[k_d], kv.at[k_d], "kvc", d, core_dev)
    for d in (0, 1, 3, 2):
        arrived(kv.at[x_at(4 - d) * 2 + other], "kvc", d)

    lanes = lane_block((128, 128))
    for g in range(2):
        for a in range(4):
            q_a = jnp.where(lanes == a, qd[0, g].astype(f32), 0.0).astype(bf16)
            do_a = jnp.where(lanes == a, qd[1, g].astype(f32), 0.0).astype(bf16)
            raw_s[g * 4 + a] = nt(q_a, kv[:, 0, g].reshape(1024, 128))
            raw_p[g * 4 + a] = nt(do_a, kv[:, 1, g].reshape(1024, 128))

    for d in range(1, 8):
        arrived(bias.at[y_at(8 - d)], "ya", d)

    spot = lax.broadcasted_iota(jnp.int32, (1, 1024), 1)
    spot_c = (lax.div(spot, 256) * 8 + lax.rem(lax.div(spot, 32), 4) * 2
              + lax.rem(lax.div(spot, 128), 2))
    keep = spot_c * 32 + lax.rem(spot, 32) < length[0]
    for b in range(8):
        bias_f[:, b * 128:(b + 1) * 128] = bias[b].reshape(128, 128).astype(f32)
    dbias[...] = jnp.zeros_like(dbias)
    att[...] = jnp.zeros_like(att)
    dqkv[0] = jnp.zeros_like(dqkv[0])

    def cores_summed(g):
        arrived(dkv_c.at[g], "dkvc", g)
        for b in range(4):
            dkv_m[g, b] = (dkv_send[core, g, b].astype(f32) + dkv_c[g, b].astype(f32)).astype(bf16)
        for d in (1, 3, 2):
            send(dkv_m.at[g, x_at(d)], dkv_in.at[g, d], "dr", g * 4 + d, x_dev(d))

    for g in range(2):
        for a in range(4):
            own = lanes == a
            do_f = jnp.where(own, qd[1, g].astype(f32), 0.0)
            logits = jnp.where(keep, raw_s[g * 4 + a] + bias_f[...], NEG)
            top = jnp.max(logits, axis=-1, keepdims=True)
            expo = jnp.exp(logits - top)
            inv = 1.0 / jnp.sum(expo, axis=-1, keepdims=True)
            out = nn(expo.astype(bf16), kv[:, 1, g].reshape(1024, 128)) * inv
            out = jnp.where(own, out, 0.0)
            att[g] = att[g] + out
            delta = jnp.sum(do_f * out, axis=-1, keepdims=True)
            shares = expo * inv
            grads = shares * (raw_p[g * 4 + a] - delta)
            for b in range(8):
                dbias[b] = dbias[b] + grads[:, b * 128:(b + 1) * 128]
            grads_s[g * 4 + a] = grads.astype(bf16)
            shares_s[g * 4 + a] = shares.astype(bf16)

    for b in range(8):
        db_send[b] = dbias[b].astype(bf16)
    for d in (4, 3, 5, 2, 6, 1, 7):
        send(db_send.at[y_at(d)], db_y.at[d], "yr", d, y_dev(d))
    for d in (1, 3, 2):
        rows_d = pl.ds(pl.multiple_of(z_at(d) * 32, 32), 32)
        send(att.at[:, rows_d, :], o_in.at[z], "oz", d, z_dev(d))
    o_in[z] = att[:, z_rows, :]

    for g in range(2):
        for a in range(4):
            if (g, a) == (1, 2):
                cores_summed(0)
            grads = grads_s[g * 4 + a]
            part = slice(a * 32, (a + 1) * 32)
            dk = nn(qdt[0, g, part, :], grads).astype(bf16)
            dv = nn(qdt[1, g, part, :], shares_s[g * 4 + a]).astype(bf16)
            for b in range(8):
                dkv_send[b % 2, g, b // 2, 0, part, :] = dk[:, b * 128:(b + 1) * 128]
                dkv_send[b % 2, g, b // 2, 1, part, :] = dv[:, b * 128:(b + 1) * 128]
        send(dkv_send.at[other, g], dkv_c.at[g], "dkvc", g, core_dev)
    for g in range(2):
        for a in range(4):
            dq = nn(grads_s[g * 4 + a], kv[:, 0, g].reshape(1024, 128)) * (32 ** (-0.5))
            dqkv[0, g] = jnp.where(lanes == a, dq, dqkv[0, g].astype(f32)).astype(bf16)
    for d in (1, 3, 2):
        rows_d = pl.ds(pl.multiple_of(z_at(d) * 32, 32), 32)
        send(dqkv.at[0, :, rows_d, :], e_in.at[z, 0], "dqz", d, z_dev(d))
    e_in[z, 0] = dqkv[0, :, z_rows, :]
    cores_summed(1)

    total = dbias[y]
    for d in range(1, 8):
        arrived(db_y.at[d], "yr", d)
        total = total + db_y[d].astype(f32)
    db_s[...] = total.reshape(2, 64, 128).astype(bf16)
    turn_own(db_s.at[core], db_t.at[core], "dt", core, by_row(core))
    send(db_s.at[other], db_t.at[core], "dt", 1, by_row(other), core)

    for g in range(2):
        for d in (1, 3, 2):
            arrived(dkv_in.at[g, d], "dr", g * 4 + d)
        for n in range(2):
            total = dkv_m[g, x, n].astype(f32)
            for d in (1, 2, 3):
                total = total + dkv_in[g, d, n].astype(f32)
            dqkv[1 + n, g] = total.T.astype(bf16)
    for d in (1, 3, 2):
        rows_d = pl.ds(pl.multiple_of(z_at(d) * 32, 32), 32)
        send(dqkv.at[1:3, :, rows_d, :], e_in.at[z, 1:3], "dkvz", d, z_dev(d))
    e_in[z, 1:3] = dqkv[1:3, :, z_rows, :]

    arrived(db_t.at[0], "dt", 0)
    arrived(db_t.at[1], "dt", 1)
    for e in range(2):
        final = db_t[:, e * 32:(e + 1) * 32, :].astype(f32).reshape(64, 128)
        outs = lane_swap([final[q * 16:(q + 1) * 16] for q in range(4)])
        for b in range(4):
            db_out[e, b] = outs[b]
    for e, d in AROUND[1:]:
        send(db_out.at[lax.rem(zhi + e, 2), z_at(d)], db_in.at[zhi, z], "dbz", e * 4 + d,
             zz_dev(e, d))
    db_in[zhi, z] = db_out[zhi, z]

    for d in (1, 2, 3):
        h_d = z_at(4 - d)
        arrived(o_in.at[h_d], "oz", d)
        arrived(e_in.at[h_d, 0], "dqz", d)
    gated = []
    pres = []
    for g in range(2):
        outs = lane_swap([o_in[h, g] for h in range(4)])
        for i in range(4):
            at = slice((g * 4 + i) * 32, (g * 4 + i + 1) * 32)
            gate_t, gg_t = gate_s[at], gg_s[at]
            gated.append((gate_t * outs[i]).astype(bf16))
            pres.append((gg_t * outs[i] * gate_t * (1.0 - gate_t)).astype(bf16))
    update_s[...] = nn(jnp.concatenate(gated, axis=0), w_out[...]).astype(bf16).reshape(8, 32, 128)
    update_out = pltpu.make_async_copy(update_s, update, leave_sem.at[4])
    update_out.start()
    for d in (1, 2, 3):
        arrived(e_in.at[z_at(4 - d), 1:3], "dkvz", d)
    sides = [jnp.concatenate(pres, axis=0)]
    for n in range(3):
        tiles = []
        for g in range(2):
            tiles += lane_swap([e_in[h, n, g].astype(f32) for h in range(4)])
        sides.append(jnp.concatenate(tiles, axis=0).astype(bf16))
    grad_window = (nt(sides[1], w_query[...]) + nt(sides[2], w_key[...])
                   + nt(sides[3], w_value[...]) + nt(sides[0], w_gate[...]))
    gw[0:8] = grad_window.reshape(8, 32, 128)
    gw[8:16] = jnp.zeros((8, 32, 128), f32)

    for copy in sent[:-7]:
        copy.wait_send()
    for e, d in AROUND[1:]:
        arrived(db_in.at[lax.rem(zhi + e, 2), z_at(4 - d)], "dbz", e * 4 + d)
    flat = (db_in[0] + db_in[1]).reshape(64, 128).T
    high = flat.astype(bf16)
    rest = flat - high.astype(f32)
    mid = rest.astype(bf16)
    low = (rest - mid.astype(f32)).astype(bf16)

    def leave(i):
        part = pl.ds(i * 4, 4)
        return pltpu.make_async_copy(result_s.at[:, part], pair_grad.at[:, part], leave_sem.at[i])

    def final_step(i, carry):
        for u in range(4):
            jj = i * 4 + u
            chosen = jnp.where(row_in == jj, w_rows[...].astype(f32), 0.0).astype(bf16)
            grad = nn(high, chosen) + (nn(mid, chosen) + nn(low, chosen))
            grad = jnp.concatenate([grad[0:32] + gw[jj], grad[32:]], axis=0) * gain_v
            hat = xhat[jj]
            first = jnp.mean(grad, axis=-1, keepdims=True)
            second = jnp.mean(grad * hat, axis=-1, keepdims=True)
            result = rstd_all[jj] * (grad - first - hat * second)
            for q in range(4):
                result_s[q, jj] = result[q * 32:(q + 1) * 32]
        leave(i).start()
        return carry

    lax.fori_loop(0, 4, final_step, 0)
    for i in range(4):
        leave(i).wait()
    update_out.wait()

    for copy in sent[-7:]:
        copy.wait_send()

    @pl.when(jnp.logical_not(stays))
    def _():
        for copy in turned:
            copy.wait_send()


def hand_over(update, pair_grad, update_out, pair_grad_out, sems):
    copies = [pltpu.make_async_copy(update, update_out, sems.at[8])]
    for q in range(4):
        for n in range(2):
            part = pl.ds(n * 8, 8)
            copies.append(pltpu.make_async_copy(
                pair_grad.at[q, part], pair_grad_out.at[q, part], sems.at[q * 2 + n]))
    for copy in copies:
        copy.start()
    for copy in copies:
        copy.wait()


def body(pair, length, ln_gain, w_query, w_key, w_value, w_gate, w_bias, w_out, out_grad):
    vmem = pl.BlockSpec(memory_space=pltpu.VMEM)
    hbm = pl.BlockSpec(memory_space=pltpu.HBM)
    smem = pl.BlockSpec(memory_space=pltpu.SMEM)

    scratch = [
        pltpu.VMEM(pair.shape, bf16),
        *[pltpu.VMEM((128, 128), bf16) for _ in range(5)],
        pltpu.VMEM(out_grad.shape, bf16),
        pltpu.SemaphoreType.DMA((7,)),
        pltpu.VMEM((16, 128, 128), f32),
        pltpu.VMEM((16, 128, 128), f32),
        pltpu.VMEM((64, 128), bf16),
        pltpu.VMEM((256, 128), f32),
        pltpu.VMEM((256, 128), f32),
        pltpu.VMEM((4, 4, 2, 32, 128), bf16),
        pltpu.VMEM((8, 2, 2, 128, 128), bf16),
        pltpu.VMEM((2, 2, 128, 128), bf16),
        pltpu.VMEM((2, 2, 128, 128), bf16),
        pltpu.VMEM((4, 16, 128), bf16),
        pltpu.VMEM((2, 2, 4, 16, 128), bf16),
        pltpu.VMEM((8, 2, 2, 32, 128), bf16),
        pltpu.VMEM((128, 1024), f32),
        pltpu.VMEM((8, 128, 128), f32),
        pltpu.VMEM((2, 128, 128), f32),
        pltpu.VMEM((3, 2, 128, 128), bf16),
        pltpu.VMEM((8, 128, 128), bf16),
        pltpu.VMEM((8, 128, 128), bf16),
        pltpu.VMEM((2, 64, 128), bf16),
        pltpu.VMEM((2, 64, 128), bf16),
        pltpu.VMEM((2, 4, 16, 128), f32),
        pltpu.VMEM((2, 4, 16, 128), f32),
        pltpu.VMEM((2, 2, 4, 2, 128, 128), bf16),
        pltpu.VMEM((2, 4, 2, 128, 128), bf16),
        pltpu.VMEM((2, 4, 2, 128, 128), bf16),
        pltpu.VMEM((2, 4, 2, 128, 128), bf16),
        pltpu.VMEM((4, 3, 2, 32, 128), bf16),
        pltpu.VMEM((4, 2, 32, 128), f32),
        pltpu.VMEM((16, 32, 128), f32),
        pltpu.VMEM((8, 128, 1024), f32),
        pltpu.VMEM((8, 128, 1024), f32),
        pltpu.VMEM((8, 128, 1024), bf16),
        pltpu.VMEM((8, 128, 1024), bf16),
        pltpu.VMEM((4, 16, 32, 128), f32),
        pltpu.SemaphoreType.DMA((5,)),
        pltpu.VMEM(out_grad.shape, bf16),
    ]
    for _, n in COPIES:
        scratch += [pltpu.SemaphoreType.DMA((n,)), pltpu.SemaphoreType.DMA((n,))]
    call = pl.pallas_call(
        kernel,
        out_shape=(
            jax.ShapeDtypeStruct(out_grad.shape, bf16),
            jax.ShapeDtypeStruct((4, 16, 32, 128), f32),
        ),
        in_specs=[hbm, smem, vmem, hbm, hbm, hbm, hbm, vmem, hbm, hbm],
        out_specs=(hbm, hbm),
        scratch_shapes=scratch,
        compiler_params=pltpu.CompilerParams(
            collective_id=0, has_side_effects=True, vmem_limit_bytes=63 * 1024 * 1024
        ),
    )
    update, pair_grad = call(
        pair, length, ln_gain.reshape(1, 128), w_query, w_key, w_value, w_gate, w_bias.T, w_out,
        out_grad,
    )
    update, pair_grad = pl.pallas_call(
        hand_over,
        out_shape=(
            jax.ShapeDtypeStruct(update.shape, bf16),
            jax.ShapeDtypeStruct(pair_grad.shape, f32),
        ),
        in_specs=[hbm, hbm],
        out_specs=(hbm, hbm),
        scratch_shapes=[pltpu.SemaphoreType.DMA((9,))],
        compiler_params=pltpu.CompilerParams(vmem_limit_bytes=63 * 1024 * 1024),
    )(update, pair_grad)
    return update, pair_grad.reshape(pair.shape)


def solution(mesh):
    tiled = P("rows", "cols", None)
    placed = (tiled, P(), P(), P(), P(), P(), P(), P(), P(), tiled)
    return jax.shard_map(
        body, mesh=mesh, in_specs=placed, out_specs=(tiled, tiled), check_vma=False
    )
```
